256 devices in a mesh: gx: 16 (over x, y_hi, core), gy: 16 (over y_lo, z).
Axes of the slice: x: 4, y: 4 (y_hi: 2, y_lo: 2; y = y_hi * 2 + y_lo), z: 8, core: 2. Of those that a mesh axis runs over, the one named last changes fastest.
Arguments:
- offsets: float32 [3, 16, 16, 64, 128], P(None, 'gx', 'gy'), may hold values from 0 to 2
- velocities: float32 [3, 16, 16, 64, 128], P(None, 'gx', 'gy'), may hold values from -5 to 5
- density: float32 [16, 16, 64, 128], P('gx', 'gy'), may hold values from 0.97 to 1.03
- tile_count: int32 [16, 16, 64], P('gx', 'gy'), may hold values from 0 to 128, as said below
- pair_tiles: int32 [2, 227072], P(None, ('gx', 'gy')), may hold values from 0 to 16383, as said below
- pair_count: int32 [256], P(('gx', 'gy')), may hold values from 1 to 887
Outputs:
- acceleration: float32 [3, 16, 16, 64, 128], P(None, 'gx', 'gy')
- density_rate: float32 [16, 16, 64, 128], P('gx', 'gy')
The draws below stay inside these ranges and needn't reach their ends.
Inputs may be any that keep to these rules, and one draw needn't show every extreme that they name: `tile_count`: empty tiles hold no particles; in every column the tiles above the surface are empty and some tile is full in every draw. `pair_tiles`: slots s of device s // 887 of gx+gy: a live pair's first tile lies in that device's column (i, j); its second lies at most one level away in column (i, j) at the same or the next level, or in column (i, j+1), (i+1, j-1), (i+1, j) or (i+1, j+1), the first index modulo 16. Every such pair of two non-empty tiles is listed exactly once, live slots first; slots after the live ones hold the device's lowest tile twice.
All inputs are finite; a program needn't handle non-finite values.
Results may differ from the reference program's by a relative error of at most 0.0003.
Values sent between devices are 32-bit elements; how exact they have to be, the bound alone decides.
No kernel may reach another device: no remote copies, remote signals or barrier semaphores. Data moves between devices by JAX's collectives and lax.ppermute only.
A program may use at most 64 MiB of HBM per device.

```python
import math
import jax
import jax.numpy as jnp
import numpy as np
from jax import lax

TILE = 128
TZ = 64
COLS_X = 16
COLS_Y = 16
PAIRS_DEV = 887


NEIGHBOUR_STEPS = np.array([[0, 0, 0], [0, 0, 1], [0, 1, -1], [0, 1, 0], [0, 1, 1], [1, -1, -1], [1, -1, 0], [1, -1, 1], [1, 0, -1], [1, 0, 0], [1, 0, 1], [1, 1, -1], [1, 1, 0], [1, 1, 1]], np.int32)


def layout(key):
    crest = jax.random.randint(jax.random.fold_in(key, 11), (), 0, COLS_X, dtype=jnp.int32)
    depth_fill = jax.random.randint(jax.random.fold_in(key, 12), (COLS_X, COLS_Y), 1, TZ // 2 + 1, dtype=jnp.int32)
    columns = jnp.arange(COLS_X, dtype=jnp.int32)
    at_crest = (columns == crest) | (columns == (crest + 1) % COLS_X)
    depth_fill = jnp.where(at_crest[:, None], TZ, depth_fill)
    packed = jax.random.randint(jax.random.fold_in(key, 13), (COLS_X, COLS_Y, TZ), 96, TILE + 1, dtype=jnp.int32)
    surface = jax.random.randint(jax.random.fold_in(key, 14), (COLS_X, COLS_Y, TZ), 1, TILE + 1, dtype=jnp.int32)
    level = jnp.arange(TZ, dtype=jnp.int32)[None, None, :]
    top = depth_fill[:, :, None] - 1
    counts = jnp.where(level < top, packed, jnp.where(level == top, surface, 0))
    counts = counts.at[crest, 0, 0].set(TILE)
    steps = jnp.asarray(NEIGHBOUR_STEPS)
    shape = (COLS_X, COLS_Y, TZ, 14)
    first_x = jnp.broadcast_to(columns[:, None, None, None], shape)
    first_y = jnp.broadcast_to(jnp.arange(COLS_Y, dtype=jnp.int32)[None, :, None, None], shape)
    first_z = jnp.broadcast_to(jnp.arange(TZ, dtype=jnp.int32)[None, None, :, None], shape)
    second_x = (first_x + steps[:, 0]) % COLS_X
    second_y = first_y + steps[:, 1]
    second_z = first_z + steps[:, 2]
    inside = (second_y >= 0) & (second_y < COLS_Y) & (second_z >= 0) & (second_z < TZ)
    second_y = jnp.clip(second_y, 0, COLS_Y - 1)
    second_z = jnp.clip(second_z, 0, TZ - 1)
    valid = inside & (counts[first_x, first_y, first_z] > 0) & (counts[second_x, second_y, second_z] > 0)
    first_id = ((first_x * COLS_Y + first_y) * TZ + first_z).reshape(COLS_X, COLS_Y, TZ * 14)
    second_id = ((second_x * COLS_Y + second_y) * TZ + second_z).reshape(COLS_X, COLS_Y, TZ * 14)
    valid = valid.reshape(COLS_X, COLS_Y, TZ * 14).astype(jnp.int32)
    score = (1 - valid) * (TZ * 14) + jnp.arange(TZ * 14, dtype=jnp.int32)
    order = jnp.argsort(score, axis=-1)[..., :PAIRS_DEV]
    number = jnp.sum(valid, axis=-1).astype(jnp.int32)
    lowest = first_id[..., :1]
    live = jnp.arange(PAIRS_DEV, dtype=jnp.int32)[None, None, :] < number[..., None]
    chosen_first = jnp.where(live, jnp.take_along_axis(first_id, order, axis=-1), lowest)
    chosen_second = jnp.where(live, jnp.take_along_axis(second_id, order, axis=-1), lowest)
    return (counts, chosen_first, chosen_second, number)


def draw_tile_count(key, part):
    counts, chosen_first, chosen_second, number = layout(key)
    return counts.astype(jnp.int32)


def draw_pair_tiles(key, part):
    counts, chosen_first, chosen_second, number = layout(key)
    return jnp.stack([chosen_first.reshape(-1), chosen_second.reshape(-1)]).astype(jnp.int32)


def draw_pair_count(key, part):
    counts, chosen_first, chosen_second, number = layout(key)
    return number.reshape(-1).astype(jnp.int32)


def steps_of(rng, dims, pieces, low, high):
    gain = 1.0
    for axis_at, blocks in pieces:
        draws = jax.random.uniform(jax.random.fold_in(jax.random.fold_in(rng, 6), axis_at), (blocks,), jnp.float32, low / len(pieces), high / len(pieces))
        gain = gain * jnp.repeat(jnp.exp(draws), dims[axis_at] // blocks).reshape((-1,) + (1,) * (len(dims) - 1 - axis_at))
    return gain


def normal_values(rng, dims, deviation, most, split=(), kind=jnp.bfloat16):
    loudness = steps_of(rng, dims, split, -0.22, 0.18) if split else 1.0
    drawn = jax.random.normal(rng, dims, jnp.float32) * deviation * loudness
    return jnp.minimum(jnp.maximum(drawn, -most), most).astype(kind)


def setup_inputs(seed: int = 0) -> dict:
    key_of = jax.random.split(jax.random.key(seed), 7)
    return {
        "offsets": jnp.clip(2.0 * jax.random.uniform(key_of[0], (3, COLS_X, COLS_Y, TZ, TILE), jnp.float32) ** steps_of(key_of[0], (3, COLS_X, COLS_Y, TZ, TILE), ((1, 16), (2, 16)), -0.2, 0.2), 0.0, 2.0),
        "velocities": normal_values(key_of[1], (3, COLS_X, COLS_Y, TZ, TILE), 1.0, 5.0, ((1, 16), (2, 16)), jnp.float32),
        "density": jnp.clip(0.97 + 0.059999943 * jax.random.uniform(key_of[2], (COLS_X, COLS_Y, TZ, TILE), jnp.float32) ** steps_of(key_of[2], (COLS_X, COLS_Y, TZ, TILE), ((0, 16), (1, 16)), -0.2, 0.2), 0.97, 1.03),
        "tile_count": draw_tile_count(jax.random.fold_in(key_of[6], 71), 0),
        "pair_tiles": draw_pair_tiles(jax.random.fold_in(key_of[6], 71), 0),
        "pair_count": draw_pair_count(jax.random.fold_in(key_of[6], 71), 0),
    }


SMOOTH = 1.0
CELL_EDGE = 2.0
MASS = 0.0625
SOUND = 5.0
BULK = SOUND * SOUND / 7.0
VISCOSITY = 0.1
KERNEL = -105.0 / (16.0 * math.pi)

def stress(values):
    pressure = BULK * (values ** 7 - 1.0)
    return pressure / (values * values)

def pair_terms(tile_a, tile_b, shift):
    spacing = tile_a[0:3, :, None] - tile_b[0:3, None, :] - shift[:, None, None]
    dist_sq = lax.optimization_barrier(jnp.sum(spacing * spacing, axis=0))
    reach = jnp.maximum(1.0 - 0.5 * jnp.sqrt(dist_sq) / SMOOTH, 0.0)
    weight = MASS * KERNEL * reach * reach * reach * tile_a[7][:, None] * tile_b[7][None, :]
    motion = tile_a[3:6, :, None] - tile_b[3:6, None, :]
    closing = lax.optimization_barrier(jnp.sum(motion * spacing, axis=0))
    mean_density = 0.5 * (tile_a[6][:, None] + tile_b[6][None, :])
    viscous = -VISCOSITY * SOUND * SMOOTH * jnp.minimum(closing, 0.0) / ((dist_sq + 0.01 * SMOOTH * SMOOTH) * mean_density)
    strength = (stress(tile_a[6])[:, None] + stress(tile_b[6])[None, :] + viscous) * weight
    thrust = strength[None] * spacing
    change = weight * closing
    forward = jnp.concatenate([-lax.optimization_barrier(jnp.sum(thrust, axis=2)), lax.optimization_barrier(jnp.sum(change, axis=1))[None]], 0)
    backward = jnp.concatenate([lax.optimization_barrier(jnp.sum(thrust, axis=1)), lax.optimization_barrier(jnp.sum(change, axis=0))[None]], 0)
    return (forward, backward)

def tile_shift(first, second):
    first_x = first // (COLS_Y * TZ)
    second_x = second // (COLS_Y * TZ)
    first_y = first // TZ % COLS_Y
    second_y = second // TZ % COLS_Y
    step_x = (second_x - first_x) % COLS_X
    step_x = jnp.where(step_x > COLS_X // 2, step_x - COLS_X, step_x)
    steps = jnp.stack([step_x, second_y - first_y, second % TZ - first % TZ])
    return CELL_EDGE * steps.astype(jnp.float32)

def reference(offsets, velocities, density, tile_count, pair_tiles, pair_count):
    tiles_total = COLS_X * COLS_Y * TZ
    mask = (jnp.arange(TILE)[None, None, None, :] < tile_count[..., None]).astype(jnp.float32)
    table = jnp.concatenate([offsets.reshape(3, tiles_total, TILE), velocities.reshape(3, tiles_total, TILE), density.reshape(1, tiles_total, TILE), mask.reshape(1, tiles_total, TILE)], 0)
    total = pair_tiles.shape[1]
    slots = jnp.arange(total)
    live = slots % PAIRS_DEV < pair_count[slots // PAIRS_DEV]
    extra = -total % 32
    first = jnp.concatenate([pair_tiles[0], jnp.zeros((extra,), pair_tiles.dtype)]).reshape(-1, 32)
    second = jnp.concatenate([pair_tiles[1], jnp.zeros((extra,), pair_tiles.dtype)]).reshape(-1, 32)
    live = jnp.concatenate([live, jnp.zeros((extra,), bool)]).reshape(-1, 32)

    def advance(accum, inputs):
        index_a, index_b, active = inputs
        shifts = tile_shift(index_a, index_b)
        forward, backward = jax.vmap(pair_terms, in_axes=(1, 1, 1))(jnp.take(table, index_a, axis=1), jnp.take(table, index_b, axis=1), shifts)
        keep = active.astype(jnp.float32)
        keep_b = keep * (index_a != index_b).astype(jnp.float32)
        accum = accum.at[:, index_a].add(jnp.transpose(forward * keep[:, None, None], (1, 0, 2)))
        accum = accum.at[:, index_b].add(jnp.transpose(backward * keep_b[:, None, None], (1, 0, 2)))
        return (accum, None)
    accum = lax.scan(advance, jnp.zeros((4, tiles_total, TILE), jnp.float32), (first, second, live))[0]
    acceleration = accum[0:3].reshape(3, COLS_X, COLS_Y, TZ, TILE)
    density_rate = accum[3].reshape(COLS_X, COLS_Y, TZ, TILE)
    return (acceleration, density_rate)
```

```python
import functools
import math

import jax
import jax.numpy as jnp
from jax import lax
from jax.experimental import pallas as pl
from jax.experimental.pallas import tpu as pltpu
from jax.sharding import PartitionSpec as P

CELL = 2.0
BULK = 25.0 / 7.0
SCALE = 0.0625 * -105.0 / (16.0 * math.pi)
EPS = 0.01
FAR = 1024.0

GROUP = 8
COLS = 5
SPAN = 10
STEPS = ((0, 0), (0, 1), (1, -1), (1, 0), (1, 1))
UNROLL = 8

POS, VEL, SQ, VDOTR, ONE = 0, 3, 6, 7, 8
DIST, CLOSE, SUMS, LEFT, FLAT = range(5)


def split(x):
    high = x.astype(jnp.bfloat16)
    rest = x - high.astype(jnp.float32)
    mid = rest.astype(jnp.bfloat16)
    low = (rest - mid.astype(jnp.float32)).astype(jnp.bfloat16)
    return high, mid, low


def stress(rho):
    cube = rho * rho * rho
    return BULK * (cube * cube * rho - 1.0) / (rho * rho)


def kernel(width, depth, codes, top_ref, blocks_ref, c0, c1, c2, c3, c4,
           o0, o1, o2, o3, o4, stage, left, right, rows, flat_a, flat_b, fsum, gsum, crow, ccol,
           grid0, grid1, high0, high1, low0, low1):
    columns = (c0, c1, c2, c3, c4)
    outs = (o0, o1, o2, o3, o4)
    groups = depth // GROUP
    top = top_ref[0]
    f32 = jnp.float32

    zero = jnp.zeros((8, width), f32)
    one = jnp.ones((8, width), f32)
    for out in outs:
        out[...] = jnp.zeros(out.shape, f32)

    def put(block, row, value):
        stage[pl.ds((block * 16 + row) * 8, 8), :] = value

    for block in range(5):
        for row in range(16):
            put(block, row, zero)
    put(DIST, SQ, one * 0.25)
    put(CLOSE, VDOTR, -one)
    put(SUMS, 9, one)
    put(LEFT, ONE, one)

    rank = lax.broadcasted_iota(jnp.int32, (8, width), 0).astype(f32)

    def place(column, step, g, half):
        at = pl.ds(pl.multiple_of(g * 8 + half * 8, 8), 8)
        x = column[0, at, :] + (CELL * step[0] - 1.0)
        y = column[1, at, :] + (CELL * step[1] - 1.0)
        z = column[2, at, :] + (CELL * (rank + (half * 8 - 1.0)) - CELL * GROUP / 2)
        return x, y, z

    def prepare(g, carry):
        clear = jnp.zeros((COLS * 16, 16, width), f32)
        gsum[pl.ds(g * (COLS * 16), COLS * 16)] = clear
        ccol[pl.ds(g * (COLS * 16), COLS * 16)] = clear[:, 0:8]
        fsum[pl.ds(g * 8, 8)] = clear[0:8]
        for k in range(8):
            crow[g * 8 + k] = jnp.zeros((width, width), f32)
        for c in range(COLS):
            for half in range(2):
                at = pl.ds(pl.multiple_of(g * 8 + half * 8, 8), 8)
                x, y, z = place(columns[c], STEPS[c], g, half)
                vx, vy, vz, rho, alive = [columns[c][n, at, :] for n in range(3, 8)]
                there = alive > 0.0
                square = x * x + y * y + z * z
                along = vx * x + vy * y + vz * z
                for n, (p, v) in enumerate(((x, vx), (y, vy), (z, vz))):
                    put(DIST, POS + n, -0.5 * p)
                    put(CLOSE, POS + n, v)
                    put(CLOSE, VEL + n, p)
                    high = p.astype(jnp.bfloat16).astype(f32)
                    mid = (p - high).astype(jnp.bfloat16).astype(f32)
                    put(SUMS, n, high)
                    put(SUMS, 3 + n, mid)
                    put(SUMS, 6 + n, p - high - mid)
                put(DIST, ONE, jnp.where(there, 0.25 * square, FAR))
                put(CLOSE, ONE, -along)
                push = stress(rho)
                put(FLAT, 0, 4.0 * rho)
                put(FLAT, 1, push)
                if c == 0:
                    for n, (p, v) in enumerate(((x, vx), (y, vy), (z, vz))):
                        put(LEFT, POS + n, p)
                        put(LEFT, VEL + n, v)
                    put(LEFT, SQ, jnp.where(there, square, 4.0 * FAR))
                    put(LEFT, VDOTR, along)
                for k in range(8 if half == 0 else 2):
                    slot = (g * COLS + c) * SPAN + half * 8 + k
                    high, mid, low = split(stage[pl.ds(k, 32, stride=8), :])
                    right[slot, 0] = high
                    right[slot, 1] = mid
                    right[slot, 2] = low
                    rows[slot] = stage[pl.ds(SUMS * 128 + k, 16, stride=8), :].astype(jnp.bfloat16)
                    sums = [stage[pl.ds(FLAT * 128 + row * 8 + k, 1), :] for row in range(2)]
                    for row in range(2):
                        flat_b[slot, row * 8:row * 8 + 8] = jnp.broadcast_to(sums[row], (8, width))
                    if c == 0 and 1 <= half * 8 + k <= 8:
                        h, m, l = [t.astype(f32) for t in split(stage[pl.ds(LEFT * 128 + k, 16, stride=8), :])]
                        wide = jnp.concatenate([h, h, h, m, m, l, m, l], 0)
                        left[g * 8 + half * 8 + k - 1] = wide.T.astype(jnp.bfloat16)
                        for row in range(2):
                            spread = jnp.broadcast_to(sums[row], (width, width)).T
                            flat_a[g * 8 + half * 8 + k - 1, row * width:row * width + width] = spread
        return carry

    lax.fori_loop(0, top, prepare, 0)

    def front(block, grids):
        for u in range(UNROLL):
            n = (block + 1) * UNROLL + u
            slot_a, slot_b = codes[0, n], codes[1, n]
            pieces = []
            for out in range(2):
                h, m, l = [right[slot_b, s, out * 16:out * 16 + 16, :] for s in range(3)]
                pieces.append(jnp.concatenate([h, m, l, h, m, h, l, m], 0))
            grids[u] = jnp.dot(left[slot_a], jnp.concatenate(pieces, 1), preferred_element_type=f32)

    def middle(block, grids, highs, lows):
        for u in range(UNROLL):
            n = (block + 1) * UNROLL + u
            slot_a, slot_b, to_a, to_b = [codes[k, n] for k in range(4)]
            rho_b = flat_b[slot_b, 0:8]
            push_b = flat_b[slot_b, 8:16]
            rho_b = jnp.concatenate([rho_b, rho_b], 0)
            push_b = jnp.concatenate([push_b, push_b], 0)
            colsum = None
            for r in range(0, width, 16):
                dist = jnp.maximum(grids[u, r:r + 16, 0:width], 1e-12)
                ncl = grids[u, r:r + 16, width:2 * width]
                denom = (dist + EPS / 4) * (flat_a[slot_a, r:r + 16] + rho_b)
                press = flat_a[slot_a, width + r:width + r + 16] + push_b
                reach = jnp.maximum(1.0 - dist * lax.rsqrt(dist), 0.0)
                weight = reach * reach * reach
                visc = jnp.maximum(ncl, 0.0) * pl.reciprocal(denom, approx=True)
                force = (press + visc) * weight
                change = ncl * weight
                high = force.astype(jnp.bfloat16)
                highs[u, r:r + 16] = high
                lows[u, r:r + 16] = (force - high.astype(f32)).astype(jnp.bfloat16)
                part = change[0:8] + change[8:16]
                colsum = part if colsum is None else colsum + part
                crow[to_a, r:r + 16, :] += change
            ccol[to_b] += colsum

    def reduce(block, highs, lows):
        for u in range(UNROLL):
            n = (block + 1) * UNROLL + u
            slot_b, to_a, to_b, own = [codes[k, n] for k in range(1, 5)]
            row_b = rows[slot_b]
            row_a = rows[own]
            high = highs[u]
            low = lows[u]
            fsum[to_a] += lax.dot_general(
                jnp.concatenate([row_b, row_b], 1), jnp.concatenate([high, low], 1),
                (((1,), (1,)), ((), ())), preferred_element_type=f32)
            gsum[to_b] += jnp.dot(
                jnp.concatenate([row_a, row_a], 1), jnp.concatenate([high, low], 0),
                preferred_element_type=f32)

    def advance(i, carry):
        front(2 * i + 1, grid1)
        middle(2 * i, grid0, high0, low0)
        reduce(2 * i - 1, high1, low1)
        front(2 * i + 2, grid0)
        middle(2 * i + 1, grid1, high1, low1)
        reduce(2 * i, high0, low0)
        return carry

    front(0, grid0)
    lax.fori_loop(0, blocks_ref[0], advance, 0)

    def finish(g, carry):
        base = g * 8
        for k in range(8):
            moved = jnp.sum(crow[base + k].T, axis=0, keepdims=True)
            stage[pl.ds(k, 1), :] = moved
        at1 = pl.ds(base + 1, 8)
        x = c0[0, at1, :] - 1.0
        y = c0[1, at1, :] - 1.0
        z = c0[2, at1, :] + (CELL * rank - CELL * GROUP / 2)

        def levels(ref, start, row):
            return jnp.concatenate([ref[start + k, row:row + 1, :] for k in range(8)], 0)

        weight = levels(fsum, base, 9)
        for n, p in enumerate((x, y, z)):
            total_n = levels(fsum, base, n) + levels(fsum, base, 3 + n) + levels(fsum, base, 6 + n)
            o0[n, at1, :] += SCALE * (total_n - p * weight)
        o0[3, at1, :] += -SCALE * stage[pl.ds(0, 8), :]
        for c in range(COLS):
            for half in range(2):
                at = pl.ds(pl.multiple_of(base + half * 8, 8), 8)
                start = (g * COLS + c) * 16 + half * 8
                place_at = place(columns[c], STEPS[c], g, half)
                weight = levels(gsum, start, 9)
                for n, p in enumerate(place_at):
                    total_n = levels(gsum, start, n) + levels(gsum, start, 3 + n) + levels(gsum, start, 6 + n)
                    outs[c][n, at, :] += SCALE * (total_n - p * weight)
                moved = jnp.concatenate([jnp.sum(ccol[start + k], axis=0, keepdims=True) for k in range(8)], 0)
                outs[c][3, at, :] += -SCALE * moved
        return carry

    lax.fori_loop(0, top, finish, 0)


def forces(pairs, live, column_x, column_y, count_y, highest, columns, depth, width):
    groups = depth // GROUP
    levels = columns[0].shape[1]
    smem = pl.BlockSpec(memory_space=pltpu.SMEM)
    vmem = pl.BlockSpec(memory_space=pltpu.VMEM)
    slots = groups * COLS * SPAN
    sums = groups * COLS * 16 + 8
    total = pairs.shape[1]
    top = highest // GROUP + 1
    level_a = pairs[0] % depth
    level_b = pairs[1] % depth
    on = (jnp.arange(total, dtype=jnp.int32) < live) & (level_a // GROUP < top)
    cell = pairs[1] // depth
    column = jnp.where(cell // count_y == column_x, 0, 3) + cell % count_y - column_y
    group = level_a // GROUP
    span = level_b + 1 - group * GROUP
    zero = jnp.zeros_like(level_a)
    codes = jnp.stack([
        jnp.where(on, level_a, zero),
        jnp.where(on, (group * COLS + column) * SPAN + span, zero),
        jnp.where(on, level_a, depth),
        jnp.where(on & (pairs[0] != pairs[1]), (group * COLS + column) * 16 + span, groups * COLS * 16),
        jnp.where(on, group * COLS * SPAN + level_a + 1 - group * GROUP, zero),
    ])
    back = 5 * UNROLL
    lead = [jnp.zeros_like(codes[k], shape=(1,)) for k in range(5)]
    lead[2] = jnp.full((1,), depth, jnp.int32)
    lead[3] = jnp.full((1,), groups * COLS * 16, jnp.int32)
    lead = jnp.stack(lead)
    codes = jnp.concatenate([
        jnp.broadcast_to(lead, (5, UNROLL)), codes, jnp.broadcast_to(lead, (5, back + (-total) % 8))], 1)
    blocks = (live + UNROLL - 1) // UNROLL
    steps = (blocks + 2) // 2
    return pl.pallas_call(
        functools.partial(kernel, width, depth),
        out_shape=[jax.ShapeDtypeStruct((4, levels, width), jnp.float32)] * COLS,
        in_specs=[smem] * 3 + [vmem] * COLS,
        out_specs=[vmem] * COLS,
        scratch_shapes=[
            pltpu.VMEM((5 * 16 * 8, width), jnp.float32),
            pltpu.VMEM((depth, width, width), jnp.bfloat16),
            pltpu.VMEM((slots, 3, 32, width), jnp.bfloat16),
            pltpu.VMEM((slots, 16, width), jnp.bfloat16),
            pltpu.VMEM((depth, 2 * width, width), jnp.float32),
            pltpu.VMEM((slots, 16, width), jnp.float32),
            pltpu.VMEM((depth + 1, 16, width), jnp.float32),
            pltpu.VMEM((sums, 16, width), jnp.float32),
            pltpu.VMEM((depth + 1, width, width), jnp.float32),
            pltpu.VMEM((sums, 8, width), jnp.float32),
        ] + [pltpu.VMEM((UNROLL, width, 2 * width), jnp.float32)] * 2
        + [pltpu.VMEM((UNROLL, width, width), jnp.bfloat16)] * 4,
        compiler_params=pltpu.CompilerParams(vmem_limit_bytes=56 * 2**20),
        name="tile_pairs",
    )(codes, top.reshape(1), steps.reshape(1), *columns)


def local(offsets, velocities, density, tile_count, pair_tiles, pair_count):
    depth, width = density.shape[2:]
    count_x = lax.axis_size("gx")
    count_y = lax.axis_size("gy")
    counts = tile_count[0, 0]
    mask = (lax.broadcasted_iota(jnp.int32, (depth, width), 1) < counts[:, None]).astype(jnp.float32)
    own = jnp.concatenate([offsets[:, 0, 0], velocities[:, 0, 0], density[0, 0][None], mask[None]], 0)
    own = jnp.pad(own, ((0, 0), (1, 7), (0, 0)))

    def device(x, y):
        return (x % count_x) * count_y + y

    def route(dx, dy):
        return [
            (device(x + dx, y + dy), device(x, y))
            for x in range(count_x)
            for y in range(count_y)
            if 0 <= y + dy < count_y
        ]

    def home(dx, dy):
        return [(target, source) for source, target in route(dx, dy)]

    columns = [own] + [lax.ppermute(own, ("gx", "gy"), route(dx, dy)) for dx, dy in STEPS[1:]]
    highest = jnp.max(jnp.where(counts > 0, jnp.arange(depth, dtype=jnp.int32), 0))
    parts = forces(
        pair_tiles, pair_count[0], lax.axis_index("gx").astype(jnp.int32),
        lax.axis_index("gy").astype(jnp.int32), count_y, highest, columns, depth, width)
    result = parts[0]
    for part, (dx, dy) in zip(parts[1:], STEPS[1:]):
        result = result + lax.ppermute(part, ("gx", "gy"), home(dx, dy))
    result = result[:, None, None, 1:depth + 1]
    return (result[0:3], result[3])


def solution(mesh):
    return jax.shard_map(
        local,
        mesh=mesh,
        in_specs=(
            P(None, "gx", "gy", None, None),
            P(None, "gx", "gy", None, None),
            P("gx", "gy", None, None),
            P("gx", "gy", None),
            P(None, ("gx", "gy")),
            P(("gx", "gy")),
        ),
        out_specs=(P(None, "gx", "gy", None, None), P("gx", "gy", None, None)),
        check_vma=False,
    )
```

```python
import functools
import math

import jax
import jax.numpy as jnp
import numpy as np
from jax import lax
from jax.experimental import pallas as pl
from jax.experimental.pallas import tpu as pltpu
from jax.sharding import PartitionSpec as P

CELL = 2.0
BULK = 25.0 / 7.0
SCALE = 0.0625 * -105.0 / (16.0 * math.pi)
EPS = 0.01
FAR = 1024.0

GROUP = 8
COLS = 5
SPAN = 10
STEPS = ((0, 0), (0, 1), (1, -1), (1, 0), (1, 1))
ACROSS = ((0, 0), (0, 1), (1, -1), (1, 0), (1, 1))
AHEAD = tuple((c, dz) for c in (2, 3, 4) for dz in (-1, 0, 1))
FIRSTS = (0, 3)
UNROLL = 8

POS, VEL, SQ, VDOTR, ONE = 0, 3, 6, 7, 8
DIST, CLOSE, SUMS, LEFT, FLAT = range(5)


def split(x):
    high = x.astype(jnp.bfloat16)
    rest = x - high.astype(jnp.float32)
    mid = rest.astype(jnp.bfloat16)
    low = (rest - mid.astype(jnp.float32)).astype(jnp.bfloat16)
    return high, mid, low


def stress(rho):
    cube = rho * rho * rho
    return BULK * (cube * cube * rho - 1.0) / (rho * rho)


def kernel(width, depth, codes, top_ref, blocks_ref, c0, c1, c2, c3, c4,
           o0, o1, o2, o3, o4, stage, left, right, rows, flat_a, flat_b, fsum, gsum, crow, ccol,
           grid0, grid1, high0, high1, low0, low1):
    columns = (c0, c1, c2, c3, c4)
    outs = (o0, o1, o2, o3, o4)
    groups = depth // GROUP
    top = top_ref[0]
    f32 = jnp.float32

    zero = jnp.zeros((8, width), f32)
    one = jnp.ones((8, width), f32)
    for out in outs:
        out[...] = jnp.zeros(out.shape, f32)

    def put(block, row, value):
        stage[pl.ds((block * 16 + row) * 8, 8), :] = value

    for block in range(5):
        for row in range(16):
            put(block, row, zero)
    put(DIST, SQ, one * 0.25)
    put(CLOSE, VDOTR, -one)
    put(SUMS, 9, one)
    put(LEFT, ONE, one)

    rank = lax.broadcasted_iota(jnp.int32, (8, width), 0).astype(f32)

    def place(column, step, g, half):
        at = pl.ds(pl.multiple_of(g * 8 + half * 8, 8), 8)
        x = column[0, at, :] + (CELL * step[0] - 1.0)
        y = column[1, at, :] + (CELL * step[1] - 1.0)
        z = column[2, at, :] + (CELL * (rank + (half * 8 - 1.0)) - CELL * GROUP / 2)
        return x, y, z

    def prepare(g, carry):
        clear = jnp.zeros((COLS * 16, 16, width), f32)
        gsum[pl.ds(g * (COLS * 16), COLS * 16)] = clear
        ccol[pl.ds(g * (COLS * 16), COLS * 16)] = clear[:, 0:8]
        for base in (0, depth):
            fsum[pl.ds(base + g * 8, 8)] = clear[0:8]
            crow[pl.ds(base + g * 8, 8)] = jnp.zeros((8, width, width), f32)
        for c in range(COLS):
            for half in range(2):
                at = pl.ds(pl.multiple_of(g * 8 + half * 8, 8), 8)
                x, y, z = place(columns[c], STEPS[c], g, half)
                vx, vy, vz, rho, alive = [columns[c][n, at, :] for n in range(3, 8)]
                there = alive > 0.0
                square = x * x + y * y + z * z
                along = vx * x + vy * y + vz * z
                for n, (p, v) in enumerate(((x, vx), (y, vy), (z, vz))):
                    put(DIST, POS + n, -0.5 * p)
                    put(CLOSE, POS + n, v)
                    put(CLOSE, VEL + n, p)
                    high = p.astype(jnp.bfloat16).astype(f32)
                    mid = (p - high).astype(jnp.bfloat16).astype(f32)
                    put(SUMS, n, high)
                    put(SUMS, 3 + n, mid)
                    put(SUMS, 6 + n, p - high - mid)
                put(DIST, ONE, jnp.where(there, 0.25 * square, FAR))
                put(CLOSE, ONE, -along)
                push = stress(rho)
                put(FLAT, 0, 4.0 * rho)
                put(FLAT, 1, push)
                if c in FIRSTS:
                    for n, (p, v) in enumerate(((x, vx), (y, vy), (z, vz))):
                        put(LEFT, POS + n, p)
                        put(LEFT, VEL + n, v)
                    put(LEFT, SQ, jnp.where(there, square, 4.0 * FAR))
                    put(LEFT, VDOTR, along)
                for k in range(8 if half == 0 else 2):
                    slot = (g * COLS + c) * SPAN + half * 8 + k
                    high, mid, low = split(stage[pl.ds(k, 32, stride=8), :])
                    right[slot, 0] = high
                    right[slot, 1] = mid
                    right[slot, 2] = low
                    rows[slot] = stage[pl.ds(SUMS * 128 + k, 16, stride=8), :].astype(jnp.bfloat16)
                    sums = [stage[pl.ds(FLAT * 128 + row * 8 + k, 1), :] for row in range(2)]
                    for row in range(2):
                        flat_b[slot, row * 8:row * 8 + 8] = jnp.broadcast_to(sums[row], (8, width))
                    if c in FIRSTS and 1 <= half * 8 + k <= 8:
                        slot_a = FIRSTS.index(c) * depth + g * 8 + half * 8 + k - 1
                        h, m, l = [t.astype(f32) for t in split(stage[pl.ds(LEFT * 128 + k, 16, stride=8), :])]
                        wide = jnp.concatenate([h, h, h, m, m, l, m, l], 0)
                        left[slot_a] = wide.T.astype(jnp.bfloat16)
                        for row in range(2):
                            spread = jnp.broadcast_to(sums[row], (width, width)).T
                            flat_a[slot_a, row * width:row * width + width] = spread
        return carry

    lax.fori_loop(0, top, prepare, 0)

    def front(block, grids):
        for u in range(UNROLL):
            n = (block + 1) * UNROLL + u
            slot_a, slot_b = codes[0, n], codes[1, n]
            pieces = []
            for out in range(2):
                h, m, l = [right[slot_b, s, out * 16:out * 16 + 16, :] for s in range(3)]
                pieces.append(jnp.concatenate([h, m, l, h, m, h, l, m], 0))
            grids[u] = jnp.dot(left[slot_a], jnp.concatenate(pieces, 1), preferred_element_type=f32)

    def middle(block, grids, highs, lows):
        for u in range(UNROLL):
            n = (block + 1) * UNROLL + u
            slot_a, slot_b, to_a, to_b = [codes[k, n] for k in range(4)]
            rho_b = flat_b[slot_b, 0:8]
            push_b = flat_b[slot_b, 8:16]
            rho_b = jnp.concatenate([rho_b, rho_b], 0)
            push_b = jnp.concatenate([push_b, push_b], 0)
            colsum = None
            for r in range(0, width, 16):
                dist = jnp.maximum(grids[u, r:r + 16, 0:width], 1e-12)
                ncl = grids[u, r:r + 16, width:2 * width]
                denom = (dist + EPS / 4) * (flat_a[slot_a, r:r + 16] + rho_b)
                press = flat_a[slot_a, width + r:width + r + 16] + push_b
                reach = jnp.maximum(1.0 - dist * lax.rsqrt(dist), 0.0)
                weight = reach * reach * reach
                visc = jnp.maximum(ncl, 0.0) * pl.reciprocal(denom, approx=True)
                force = (press + visc) * weight
                change = ncl * weight
                high = force.astype(jnp.bfloat16)
                highs[u, r:r + 16] = high
                lows[u, r:r + 16] = (force - high.astype(f32)).astype(jnp.bfloat16)
                part = change[0:8] + change[8:16]
                colsum = part if colsum is None else colsum + part
                crow[to_a, r:r + 16, :] += change
            ccol[to_b] += colsum

    def reduce(block, highs, lows):
        for u in range(UNROLL):
            n = (block + 1) * UNROLL + u
            slot_b, to_a, to_b, own = [codes[k, n] for k in range(1, 5)]
            row_b = rows[slot_b]
            row_a = rows[own]
            high = highs[u]
            low = lows[u]
            fsum[to_a] += lax.dot_general(
                jnp.concatenate([row_b, row_b], 1), jnp.concatenate([high, low], 1),
                (((1,), (1,)), ((), ())), preferred_element_type=f32)
            gsum[to_b] += jnp.dot(
                jnp.concatenate([row_a, row_a], 1), jnp.concatenate([high, low], 0),
                preferred_element_type=f32)

    def advance(i, carry):
        front(2 * i + 1, grid1)
        middle(2 * i, grid0, high0, low0)
        reduce(2 * i - 1, high1, low1)
        front(2 * i + 2, grid0)
        middle(2 * i + 1, grid1, high1, low1)
        reduce(2 * i, high0, low0)
        return carry

    front(0, grid0)
    lax.fori_loop(0, blocks_ref[0], advance, 0)

    def finish(g, carry):
        base = g * 8
        at1 = pl.ds(base + 1, 8)

        def levels(ref, start, row):
            return jnp.concatenate([ref[start + k, row:row + 1, :] for k in range(8)], 0)

        for n_first, c in enumerate(FIRSTS):
            start = n_first * depth + base
            for k in range(8):
                stage[pl.ds(k, 1), :] = jnp.sum(crow[start + k].T, axis=0, keepdims=True)
            x = columns[c][0, at1, :] + (CELL * STEPS[c][0] - 1.0)
            y = columns[c][1, at1, :] + (CELL * STEPS[c][1] - 1.0)
            z = columns[c][2, at1, :] + (CELL * rank - CELL * GROUP / 2)
            weight = levels(fsum, start, 9)
            for n, p in enumerate((x, y, z)):
                total_n = levels(fsum, start, n) + levels(fsum, start, 3 + n) + levels(fsum, start, 6 + n)
                outs[c][n, at1, :] += SCALE * (total_n - p * weight)
            outs[c][3, at1, :] += -SCALE * stage[pl.ds(0, 8), :]
        for c in range(COLS):
            for half in range(2):
                at = pl.ds(pl.multiple_of(base + half * 8, 8), 8)
                start = (g * COLS + c) * 16 + half * 8
                place_at = place(columns[c], STEPS[c], g, half)
                weight = levels(gsum, start, 9)
                for n, p in enumerate(place_at):
                    total_n = levels(gsum, start, n) + levels(gsum, start, 3 + n) + levels(gsum, start, 6 + n)
                    outs[c][n, at, :] += SCALE * (total_n - p * weight)
                moved = jnp.concatenate([jnp.sum(ccol[start + k], axis=0, keepdims=True) for k in range(8)], 0)
                outs[c][3, at, :] += -SCALE * moved
        return carry

    lax.fori_loop(0, top, finish, 0)


def plan(fills, column_x, column_y, depth):
    trash_a = 2 * depth
    trash_b = (depth // GROUP) * COLS * 16
    wrapped = jnp.pad(jnp.concatenate([fills[-1:], fills, fills[:2]], 0), ((0, 0), (1, 1)))
    near = lax.dynamic_slice(wrapped, (column_x, column_y), (4, 3)).reshape(12)
    kinds = ACROSS + AHEAD

    def heights(cells):
        pick = np.zeros((len(cells), 12), np.int32)
        pick[np.arange(len(cells)), cells] = 1
        return jnp.sum(jnp.asarray(pick) * near, axis=1)

    def cell(behind, c):
        return (behind + 1 + STEPS[c][0]) * 3 + 1 + STEPS[c][1]

    def runs(firsts, seconds, rises, low, high):
        rises = np.asarray(rises, np.int32)
        low = jnp.maximum(low, np.maximum(-rises, 0))
        high = jnp.minimum(jnp.minimum(high, heights(firsts)), heights(seconds) - rises)
        return low, jnp.maximum(high - low, 0)

    offsets = (-1, 0, 1)
    _, sizes = runs(
        [cell(o, 0) for o in offsets for _ in kinds], [cell(o, c) for o in offsets for c, _ in kinds],
        [dz for _ in offsets for _, dz in kinds], 0, depth)
    work = jnp.sum(sizes.reshape(3, len(kinds)), axis=1)
    own_height, next_height = near[cell(0, 0)], near[cell(1, 0)]
    keep = own_height - jnp.minimum(jnp.maximum(work[1] - work[0], 0) // (2 * len(ACROSS)), own_height)
    keep_next = next_height - jnp.minimum(jnp.maximum(work[2] - work[1], 0) // (2 * len(ACROSS)), next_height)

    count = len(ACROSS)
    low = jnp.concatenate([jnp.zeros((len(kinds),), jnp.int32), jnp.broadcast_to(keep_next, (count,))])
    high = jnp.concatenate([jnp.broadcast_to(keep, (count,)), jnp.full((len(kinds),), depth, jnp.int32)])
    rises = [dz for _, dz in kinds + ACROSS]
    low, sizes = runs(
        [cell(0, 0)] * len(kinds) + [cell(1, 0)] * count,
        [cell(0, c) for c, _ in kinds] + [cell(1, c) for c, _ in ACROSS], rises, low, high)
    ends = jnp.cumsum(sizes)
    starts = ends - sizes
    live = ends[-1]
    static = np.asarray(
        [c * 8 + (dz + 1) * 2 for c, dz in kinds] + [(c + 3) * 8 + (dz + 1) * 2 + 1 for c, dz in ACROSS], np.int32)
    shift = low - starts
    total = 14 * depth + 6 * UNROLL
    place = jnp.arange(total, dtype=jnp.int32) - UNROLL
    reached = (place[None, :] >= starts[:, None]).astype(jnp.int32)
    shift = jnp.sum(reached * jnp.diff(shift, prepend=0)[:, None], axis=0)
    code = jnp.sum(reached * jnp.asarray(np.diff(static, prepend=0))[:, None], axis=0)
    on = (place >= 0) & (place < live)
    level = jnp.where(on, place + shift, 0)
    code = jnp.where(on, code, 0)
    first = code & 1
    rise = ((code >> 1) & 3) - 1
    second = code >> 3
    group = level // GROUP
    span = level + 1 - group * GROUP
    slot_a = first * depth + level
    row = group * COLS + second
    alone = (rise == 0) & (second == 3 * first)
    codes = jnp.stack([
        slot_a,
        jnp.where(on, row * SPAN + span + rise, 0),
        jnp.where(on, slot_a, trash_a),
        jnp.where(on & ~alone, row * 16 + span + rise, trash_b),
        (group * COLS + 3 * first) * SPAN + span,
    ])
    blocks = (live + UNROLL - 1) // UNROLL
    top = (jnp.maximum(own_height, jnp.where(keep_next < next_height, next_height, 0)) + GROUP - 1) // GROUP
    return codes, top.reshape(1), ((blocks + 2) // 2).reshape(1), live


def forces(codes, top, steps, columns, depth, width):
    groups = depth // GROUP
    levels = columns[0].shape[1]
    smem = pl.BlockSpec(memory_space=pltpu.SMEM)
    vmem = pl.BlockSpec(memory_space=pltpu.VMEM)
    slots = groups * COLS * SPAN
    sums = groups * COLS * 16 + 8
    return pl.pallas_call(
        functools.partial(kernel, width, depth),
        out_shape=[jax.ShapeDtypeStruct((4, levels, width), jnp.float32)] * COLS,
        in_specs=[smem] * 3 + [vmem] * COLS,
        out_specs=[vmem] * COLS,
        scratch_shapes=[
            pltpu.VMEM((5 * 16 * 8, width), jnp.float32),
            pltpu.VMEM((2 * depth, width, width), jnp.bfloat16),
            pltpu.VMEM((slots, 3, 32, width), jnp.bfloat16),
            pltpu.VMEM((slots, 16, width), jnp.bfloat16),
            pltpu.VMEM((2 * depth, 2 * width, width), jnp.float32),
            pltpu.VMEM((slots, 16, width), jnp.float32),
            pltpu.VMEM((2 * depth + 1, 16, width), jnp.float32),
            pltpu.VMEM((sums, 16, width), jnp.float32),
            pltpu.VMEM((2 * depth + 1, width, width), jnp.float32),
            pltpu.VMEM((sums, 8, width), jnp.float32),
        ] + [pltpu.VMEM((UNROLL, width, 2 * width), jnp.float32)] * 2
        + [pltpu.VMEM((UNROLL, width, width), jnp.bfloat16)] * 4,
        compiler_params=pltpu.CompilerParams(vmem_limit_bytes=60 * 2**20),
        name="tile_pairs",
    )(codes, top, steps, *columns)


def local(offsets, velocities, density, tile_count, pair_tiles, pair_count):
    depth, width = density.shape[2:]
    count_x = lax.axis_size("gx")
    count_y = lax.axis_size("gy")
    counts = tile_count[0, 0]
    mask = (lax.broadcasted_iota(jnp.int32, (depth, width), 1) < counts[:, None]).astype(jnp.float32)
    own = jnp.concatenate([offsets[:, 0, 0], velocities[:, 0, 0], density[0, 0][None], mask[None]], 0)
    own = jnp.pad(own, ((0, 0), (1, 7), (0, 0)))

    def device(x, y):
        return (x % count_x) * count_y + y

    def route(dx, dy):
        return [
            (device(x + dx, y + dy), device(x, y))
            for x in range(count_x)
            for y in range(count_y)
            if 0 <= y + dy < count_y
        ]

    def home(dx, dy):
        return [(target, source) for source, target in route(dx, dy)]

    columns = [own] + [lax.ppermute(own, ("gx", "gy"), route(dx, dy)) for dx, dy in STEPS[1:]]
    fill = jnp.max(jnp.where(counts > 0, jnp.arange(1, depth + 1, dtype=jnp.int32), 0))
    fills = lax.all_gather(fill, ("gx", "gy")).reshape(count_x, count_y)
    codes, top, steps, _ = plan(
        fills, lax.axis_index("gx").astype(jnp.int32), lax.axis_index("gy").astype(jnp.int32), depth)
    parts = forces(codes, top, steps, columns, depth, width)
    result = parts[0]
    for part, (dx, dy) in zip(parts[1:], STEPS[1:]):
        result = result + lax.ppermute(part, ("gx", "gy"), home(dx, dy))
    result = result[:, None, None, 1:depth + 1]
    return (result[0:3], result[3])


def solution(mesh):
    return jax.shard_map(
        local,
        mesh=mesh,
        in_specs=(
            P(None, "gx", "gy", None, None),
            P(None, "gx", "gy", None, None),
            P("gx", "gy", None, None),
            P("gx", "gy", None),
            P(None, ("gx", "gy")),
            P(("gx", "gy")),
        ),
        out_specs=(P(None, "gx", "gy", None, None), P("gx", "gy", None, None)),
        check_vma=False,
    )
```

```python
import functools
import math

import jax
import jax.numpy as jnp
from jax import lax
from jax.experimental import pallas as pl
from jax.experimental.pallas import tpu as pltpu
from jax.sharding import PartitionSpec as P

CELL = 2.0
BULK = 25.0 / 7.0
SCALE = 0.0625 * -105.0 / (16.0 * math.pi)
EPS = 0.01
FAR = 1024.0

GROUP = 8
COLS = 4
SPAN = 10
STEPS = ((0, 0), (0, 1), (1, 0), (1, 1))
FIRSTS = (0, 2)
ACROSS = ((0, 0, 0), (0, 0, 1), (0, 1, -1), (0, 1, 0), (0, 1, 1))
AHEAD = tuple((n, c, dz) for n, c in ((0, 2), (0, 3), (1, 1)) for dz in (-1, 0, 1))
NEXT = tuple((1, c + 2, dz) for _, c, dz in ACROSS)
NOTE = 71
UNROLL = 8

POS, VEL, SQ, VDOTR, ONE = 0, 3, 6, 7, 8
DIST, CLOSE, SUMS, LEFT, FLAT = range(5)


def split(x):
    high = x.astype(jnp.bfloat16)
    rest = x - high.astype(jnp.float32)
    mid = rest.astype(jnp.bfloat16)
    low = (rest - mid.astype(jnp.float32)).astype(jnp.bfloat16)
    return high, mid, low


def stress(rho):
    cube = rho * rho * rho
    return BULK * (cube * cube * rho - 1.0) / (rho * rho)


def kernel(width, depth, before_ref, c0, c1, c2, c3, own_force, own_rate, o1, o2, o3,
           stage, left, right, rows, flat_a, flat_b, fsum, gsum, crow, ccol,
           grid0, grid1, high0, high1, low0, low1, a0, a1, a2, a3, plans, codes, arrived):
    columns = (c0, c1, c2, c3)
    outs = (a0, a1, a2, a3)
    groups = depth // GROUP
    trash_a = 2 * depth
    trash_b = groups * COLS * 16
    f32 = jnp.float32

    def note(c, n):
        return jnp.max(columns[c][n, NOTE:NOTE + 1, :]).astype(jnp.int32)

    heights = [note(c, 0) for c in range(COLS)]
    before, here, after = before_ref[0], note(0, 1), note(2, 1)

    def kept(height, work, behind):
        return height - jnp.minimum(lax.div(jnp.maximum(work - behind, 0), 2 * len(ACROSS)), height)

    keep, keep_next = kept(heights[0], here, before), kept(heights[2], after, here)

    place = (lax.broadcasted_iota(jnp.int32, (16, 128), 0) * 128
             + lax.broadcasted_iota(jnp.int32, (16, 128), 1) - UNROLL)
    live = jnp.int32(0)
    reach = jnp.int32(0)
    level = jnp.zeros_like(place)
    code = jnp.zeros_like(place)
    for names, low, high in ((ACROSS, 0, keep), (AHEAD, 0, depth), (NEXT, keep_next, depth)):
        for n, c, dz in names:
            start = jnp.maximum(low, max(-dz, 0))
            stop = jnp.minimum(jnp.minimum(high, heights[FIRSTS[n]]), heights[c] - dz)
            some = stop > start
            here_on = place >= live
            level = jnp.where(here_on, place + (start - live), level)
            code = jnp.where(here_on, c * 8 + (dz + 1) * 2 + n, code)
            live += jnp.where(some, stop - start, 0)
            reach = jnp.where(some, jnp.maximum(reach, stop), reach)
    on = (place >= 0) & (place < live)
    level = jnp.where(on, level, 0)
    code = jnp.where(on, code, 2)
    first = code & 1
    rise = (lax.shift_right_logical(code, 1) & 3) - 1
    second = lax.shift_right_logical(code, 3)
    group = lax.shift_right_logical(level, 3)
    span = (level & (GROUP - 1)) + 1
    row = group * COLS + second
    slot_a = first * depth + level
    first_column = first * FIRSTS[1]
    alone = (rise == 0) & (second == first_column)
    plans[0] = slot_a
    plans[1] = row * SPAN + span + rise
    plans[2] = jnp.where(on, slot_a, trash_a)
    plans[3] = jnp.where(on & jnp.logical_not(alone), row * 16 + span + rise, trash_b)
    plans[4] = (group * COLS + first_column) * SPAN + span
    copy = pltpu.make_async_copy(plans, codes, arrived)
    copy.start()
    top = lax.div(reach + (GROUP - 1), GROUP)

    zero = jnp.zeros((8, width), f32)
    one = jnp.ones((8, width), f32)
    for out in outs:
        out[...] = jnp.zeros(out.shape, f32)

    def put(block, row, value):
        stage[pl.ds((block * 16 + row) * 8, 8), :] = value

    for block in range(5):
        for row in range(16):
            put(block, row, zero)
    put(DIST, SQ, one * 0.25)
    put(CLOSE, VDOTR, -one)
    put(SUMS, 9, one)
    put(LEFT, ONE, one)

    rank = lax.broadcasted_iota(jnp.int32, (8, width), 0).astype(f32)

    def place(column, step, g, half):
        at = pl.ds(pl.multiple_of(g * 8 + half * 8, 8), 8)
        x = column[0, at, :] + (CELL * step[0] - 1.0)
        y = column[1, at, :] + (CELL * step[1] - 1.0)
        z = column[2, at, :] + (CELL * (rank + (half * 8 - 1.0)) - CELL * GROUP / 2)
        return x, y, z

    def prepare(g, carry):
        clear = jnp.zeros((COLS * 16, 16, width), f32)
        gsum[pl.ds(g * (COLS * 16), COLS * 16)] = clear
        ccol[pl.ds(g * (COLS * 16), COLS * 16)] = clear[:, 0:8]
        for base in (0, depth):
            fsum[pl.ds(base + g * 8, 8)] = clear[0:8]
            crow[pl.ds(base + g * 8, 8)] = jnp.zeros((8, width, width), f32)
        for c in range(COLS):
            for half in range(2):
                at = pl.ds(pl.multiple_of(g * 8 + half * 8, 8), 8)
                x, y, z = place(columns[c], STEPS[c], g, half)
                vx, vy, vz, rho, alive = [columns[c][n, at, :] for n in range(3, 8)]
                there = alive > 0.0
                square = x * x + y * y + z * z
                along = vx * x + vy * y + vz * z
                for n, (p, v) in enumerate(((x, vx), (y, vy), (z, vz))):
                    put(DIST, POS + n, -0.5 * p)
                    put(CLOSE, POS + n, v)
                    put(CLOSE, VEL + n, p)
                    high = p.astype(jnp.bfloat16).astype(f32)
                    mid = (p - high).astype(jnp.bfloat16).astype(f32)
                    put(SUMS, n, high)
                    put(SUMS, 3 + n, mid)
                    put(SUMS, 6 + n, p - high - mid)
                put(DIST, ONE, jnp.where(there, 0.25 * square, FAR))
                put(CLOSE, ONE, -along)
                push = stress(rho)
                put(FLAT, 0, 4.0 * rho)
                put(FLAT, 1, push)
                if c in FIRSTS:
                    for n, (p, v) in enumerate(((x, vx), (y, vy), (z, vz))):
                        put(LEFT, POS + n, p)
                        put(LEFT, VEL + n, v)
                    put(LEFT, SQ, jnp.where(there, square, 4.0 * FAR))
                    put(LEFT, VDOTR, along)
                for k in range(8 if half == 0 else 2):
                    slot = (g * COLS + c) * SPAN + half * 8 + k
                    high, mid, low = split(stage[pl.ds(k, 32, stride=8), :])
                    right[slot, 0] = high
                    right[slot, 1] = mid
                    right[slot, 2] = low
                    rows[slot] = stage[pl.ds(SUMS * 128 + k, 16, stride=8), :].astype(jnp.bfloat16)
                    sums = [stage[pl.ds(FLAT * 128 + row * 8 + k, 1), :] for row in range(2)]
                    for row in range(2):
                        flat_b[slot, row * 8:row * 8 + 8] = jnp.broadcast_to(sums[row], (8, width))
                    if c in FIRSTS and 1 <= half * 8 + k <= 8:
                        slot_a = FIRSTS.index(c) * depth + g * 8 + half * 8 + k - 1
                        h, m, l = [t.astype(f32) for t in split(stage[pl.ds(LEFT * 128 + k, 16, stride=8), :])]
                        wide = jnp.concatenate([h, h, h, m, m, l, m, l], 0)
                        left[slot_a] = wide.T.astype(jnp.bfloat16)
                        for row in range(2):
                            spread = jnp.broadcast_to(sums[row], (width, width)).T
                            flat_a[slot_a, row * width:row * width + width] = spread
        return carry

    lax.fori_loop(0, top, prepare, 0)

    def fetch(fields, block, u):
        n = (block + 1) * UNROLL + u
        return [codes[k, lax.shift_right_logical(n, 7), n & 127] for k in fields]

    def front(block, grids):
        for u in range(UNROLL):
            slot_a, slot_b = fetch((0, 1), block, u)
            pieces = []
            for out in range(2):
                h, m, l = [right[slot_b, s, out * 16:out * 16 + 16, :] for s in range(3)]
                pieces.append(jnp.concatenate([h, m, l, h, m, h, l, m], 0))
            grids[u] = jnp.dot(left[slot_a], jnp.concatenate(pieces, 1), preferred_element_type=f32)

    def middle(block, grids, highs, lows):
        for u in range(UNROLL):
            slot_a, slot_b, to_a, to_b = fetch((0, 1, 2, 3), block, u)
            rho_b = flat_b[slot_b, 0:8]
            push_b = flat_b[slot_b, 8:16]
            rho_b = jnp.concatenate([rho_b, rho_b], 0)
            push_b = jnp.concatenate([push_b, push_b], 0)
            colsum = None
            for r in range(0, width, 16):
                dist = jnp.maximum(grids[u, r:r + 16, 0:width], 1e-12)
                ncl = grids[u, r:r + 16, width:2 * width]
                denom = (dist + EPS / 4) * (flat_a[slot_a, r:r + 16] + rho_b)
                press = flat_a[slot_a, width + r:width + r + 16] + push_b
                reach = jnp.maximum(1.0 - dist * lax.rsqrt(dist), 0.0)
                weight = reach * reach * reach
                visc = jnp.maximum(ncl, 0.0) * pl.reciprocal(denom, approx=True)
                force = (press + visc) * weight
                change = ncl * weight
                high = force.astype(jnp.bfloat16)
                highs[u, r:r + 16] = high
                lows[u, r:r + 16] = (force - high.astype(f32)).astype(jnp.bfloat16)
                part = change[0:8] + change[8:16]
                colsum = part if colsum is None else colsum + part
                crow[to_a, r:r + 16, :] += change
            ccol[to_b] += colsum

    def reduce(block, highs, lows):
        for u in range(UNROLL):
            slot_b, to_a, to_b, own = fetch((1, 2, 3, 4), block, u)
            row_b = rows[slot_b]
            row_a = rows[own]
            high = highs[u]
            low = lows[u]
            fsum[to_a] += lax.dot_general(
                jnp.concatenate([row_b, row_b], 1), jnp.concatenate([high, low], 1),
                (((1,), (1,)), ((), ())), preferred_element_type=f32)
            gsum[to_b] += jnp.dot(
                jnp.concatenate([row_a, row_a], 1), jnp.concatenate([high, low], 0),
                preferred_element_type=f32)

    def advance(i, carry):
        front(2 * i + 1, grid1)
        middle(2 * i, grid0, high0, low0)
        reduce(2 * i - 1, high1, low1)
        front(2 * i + 2, grid0)
        middle(2 * i + 1, grid1, high1, low1)
        reduce(2 * i, high0, low0)
        return carry

    copy.wait()
    blocks = lax.div(live + (UNROLL - 1), UNROLL)
    front(0, grid0)
    lax.fori_loop(0, lax.div(blocks + 2, 2), advance, 0)

    def finish(g, carry):
        base = g * 8
        at1 = pl.ds(base + 1, 8)

        def levels(ref, start, row):
            return jnp.concatenate([ref[start + k, row:row + 1, :] for k in range(8)], 0)

        for n_first, c in enumerate(FIRSTS):
            start = n_first * depth + base
            for k in range(8):
                stage[pl.ds(k, 1), :] = jnp.sum(crow[start + k].T, axis=0, keepdims=True)
            x = columns[c][0, at1, :] + (CELL * STEPS[c][0] - 1.0)
            y = columns[c][1, at1, :] + (CELL * STEPS[c][1] - 1.0)
            z = columns[c][2, at1, :] + (CELL * rank - CELL * GROUP / 2)
            weight = levels(fsum, start, 9)
            for n, p in enumerate((x, y, z)):
                total_n = levels(fsum, start, n) + levels(fsum, start, 3 + n) + levels(fsum, start, 6 + n)
                outs[c][n, at1, :] += SCALE * (total_n - p * weight)
            outs[c][3, at1, :] += -SCALE * stage[pl.ds(0, 8), :]
        for c in range(COLS):
            for half in range(2):
                at = pl.ds(pl.multiple_of(base + half * 8, 8), 8)
                start = (g * COLS + c) * 16 + half * 8
                place_at = place(columns[c], STEPS[c], g, half)
                weight = levels(gsum, start, 9)
                for n, p in enumerate(place_at):
                    total_n = levels(gsum, start, n) + levels(gsum, start, 3 + n) + levels(gsum, start, 6 + n)
                    outs[c][n, at, :] += SCALE * (total_n - p * weight)
                moved = jnp.concatenate([jnp.sum(ccol[start + k], axis=0, keepdims=True) for k in range(8)], 0)
                outs[c][3, at, :] += -SCALE * moved
        return carry

    lax.fori_loop(0, top, finish, 0)
    inner = slice(1, depth + 1)
    own_force[...] = a0[0:3, inner, :]
    own_rate[...] = a0[3, inner, :]
    for out, sums in ((o1, a1), (o2, a2), (o3, a3)):
        out[...] = sums[:, inner, :]


def forces(before, columns, depth, width):
    groups = depth // GROUP
    levels = columns[0].shape[1]
    smem = pl.BlockSpec(memory_space=pltpu.SMEM)
    vmem = pl.BlockSpec(memory_space=pltpu.VMEM)
    slots = groups * COLS * SPAN
    sums = groups * COLS * 16 + 8
    f32, bf16 = jnp.float32, jnp.bfloat16
    return pl.pallas_call(
        functools.partial(kernel, width, depth),
        out_shape=[jax.ShapeDtypeStruct((3, depth, width), f32), jax.ShapeDtypeStruct((depth, width), f32)]
        + [jax.ShapeDtypeStruct((4, depth, width), f32)] * (COLS - 1),
        in_specs=[smem] + [vmem] * COLS,
        out_specs=[vmem] * (COLS + 1),
        scratch_shapes=[
            pltpu.VMEM((5 * 16 * 8, width), f32),
            pltpu.VMEM((2 * depth, width, width), bf16),
            pltpu.VMEM((slots, 3, 32, width), bf16),
            pltpu.VMEM((slots, 16, width), bf16),
            pltpu.VMEM((2 * depth, 2 * width, width), f32),
            pltpu.VMEM((slots, 16, width), f32),
            pltpu.VMEM((2 * depth + 1, 16, width), f32),
            pltpu.VMEM((sums, 16, width), f32),
            pltpu.VMEM((2 * depth + 1, width, width), f32),
            pltpu.VMEM((sums, 8, width), f32),
        ] + [pltpu.VMEM((UNROLL, width, 2 * width), f32)] * 2
        + [pltpu.VMEM((UNROLL, width, width), bf16)] * 4
        + [pltpu.VMEM((4, levels, width), f32)] * COLS
        + [pltpu.VMEM((5, 16, 128), jnp.int32), pltpu.SMEM((5, 16, 128), jnp.int32), pltpu.SemaphoreType.DMA],
        compiler_params=pltpu.CompilerParams(vmem_limit_bytes=58 * 2**20),
        name="tile_pairs",
    )(before, *columns)


def local(offsets, velocities, density, tile_count, pair_tiles, pair_count):
    depth, width = density.shape[2:]
    count_x = lax.axis_size("gx")
    count_y = lax.axis_size("gy")
    counts = tile_count[0, 0]
    mask = (lax.broadcasted_iota(jnp.int32, (depth, width), 1) < counts[:, None]).astype(jnp.float32)
    height = jnp.max(jnp.where(counts > 0, jnp.arange(1, depth + 1, dtype=jnp.int32), 0)).astype(jnp.float32)
    own = jnp.concatenate([offsets[:, 0, 0], velocities[:, 0, 0], density[0, 0][None], mask[None]], 0)
    own = jnp.pad(own, ((0, 0), (1, NOTE - depth), (0, 0)))
    component = lax.broadcasted_iota(jnp.int32, own.shape, 0)
    noted = jnp.where(component == 0, height, pair_count[0].astype(jnp.float32))
    own = jnp.where(lax.broadcasted_iota(jnp.int32, own.shape, 1) == NOTE, noted, own)

    def device(x, y):
        return (x % count_x) * count_y + y

    def route(dx, dy):
        return [
            (device(x + dx, y + dy), device(x, y))
            for x in range(count_x)
            for y in range(count_y)
            if 0 <= y + dy < count_y
        ]

    def home(dx, dy):
        return [(target, source) for source, target in route(dx, dy)]

    columns = [own] + [lax.ppermute(own, ("gx", "gy"), route(dx, dy)) for dx, dy in STEPS[1:]]
    before = lax.ppermute(pair_count, ("gx", "gy"), route(-1, 0))
    force, rate, *parts = forces(before, columns, depth, width)
    parts = [lax.ppermute(part, ("gx", "gy"), home(dx, dy)) for part, (dx, dy) in zip(parts, STEPS[1:])]
    force = force + (parts[0][0:3] + parts[1][0:3] + parts[2][0:3])
    rate = rate + (parts[0][3] + parts[1][3] + parts[2][3])
    return (force[:, None, None], rate[None, None])


def solution(mesh):
    return jax.shard_map(
        local,
        mesh=mesh,
        in_specs=(
            P(None, "gx", "gy", None, None),
            P(None, "gx", "gy", None, None),
            P("gx", "gy", None, None),
            P("gx", "gy", None),
            P(None, ("gx", "gy")),
            P(("gx", "gy")),
        ),
        out_specs=(P(None, "gx", "gy", None, None), P("gx", "gy", None, None)),
        check_vma=False,
    )
```

```python
import functools
import math

import jax
import jax.numpy as jnp
from jax import lax
from jax.experimental import pallas as pl
from jax.experimental.pallas import tpu as pltpu
from jax.sharding import PartitionSpec as P

CELL = 2.0
BULK = 25.0 / 7.0
SCALE = 0.0625 * -105.0 / (16.0 * math.pi)
EPS = 0.01
FAR = 1024.0

GROUP = 8
COLS = 4
SPAN = 10
STEPS = ((0, 0), (0, 1), (1, 0), (1, 1))
FIRSTS = (0, 2)
ACROSS = ((0, 0, 0), (0, 0, 1), (0, 1, -1), (0, 1, 0), (0, 1, 1))
AHEAD = tuple((n, c, dz) for n, c in ((0, 2), (0, 3), (1, 1)) for dz in (-1, 0, 1))
NEXT = tuple((1, c + 2, dz) for _, c, dz in ACROSS)
SHARE = 7
NOTE = 71
UNROLL = 8

POS, VEL, SQ, VDOTR, ONE = 0, 3, 6, 7, 8
DIST, CLOSE, SUMS, LEFT, FLAT = range(5)


def split(x):
    high = x.astype(jnp.bfloat16)
    rest = x - high.astype(jnp.float32)
    mid = rest.astype(jnp.bfloat16)
    low = (rest - mid.astype(jnp.float32)).astype(jnp.bfloat16)
    return high, mid, low


def stress(rho):
    cube = rho * rho * rho
    return BULK * (cube * cube * rho - 1.0) / (rho * rho)


def kernel(width, depth, before_ref, c0, c1, c2, c3, own_force, own_rate, o1, o2, o3,
           stage, left, right, rows, flat_a, flat_b, fsum, gsum, crow, ccol,
           grid0, grid1, high0, high1, low0, low1, a0, a1, a2, a3, plans, codes, arrived):
    columns = (c0, c1, c2, c3)
    outs = (a0, a1, a2, a3)
    groups = depth // GROUP
    trash_a = 2 * depth
    trash_b = groups * COLS * 16
    f32 = jnp.float32

    steps_up = lax.broadcasted_iota(jnp.int32, columns[0].shape[1:], 0).astype(f32)
    heights = [jnp.max(steps_up * columns[c][7]).astype(jnp.int32) for c in range(COLS)]
    before = jnp.max(before_ref[...]).astype(jnp.int32)
    here, after = [jnp.max(columns[c][0, NOTE:NOTE + 1, :]).astype(jnp.int32) for c in FIRSTS]

    def kept(height, work, behind):
        return height - jnp.minimum(lax.div(jnp.maximum(work - behind, 0), SHARE), height)

    keep, keep_next = kept(heights[0], here, before), kept(heights[2], after, here)

    place = (lax.broadcasted_iota(jnp.int32, (16, 128), 0) * 128
             + lax.broadcasted_iota(jnp.int32, (16, 128), 1) - UNROLL)
    live = jnp.int32(0)
    reach = jnp.int32(0)
    level = jnp.zeros_like(place)
    code = jnp.zeros_like(place)
    for names, low, high in ((ACROSS, 0, keep), (AHEAD, 0, depth), (NEXT, keep_next, depth)):
        for n, c, dz in names:
            start = jnp.maximum(low, max(-dz, 0))
            stop = jnp.minimum(jnp.minimum(high, heights[FIRSTS[n]]), heights[c] - dz)
            some = stop > start
            here_on = place >= live
            level = jnp.where(here_on, place + (start - live), level)
            code = jnp.where(here_on, c * 8 + (dz + 1) * 2 + n, code)
            live += jnp.where(some, stop - start, 0)
            reach = jnp.where(some, jnp.maximum(reach, stop), reach)
    on = (place >= 0) & (place < live)
    level = jnp.where(on, level, 0)
    code = jnp.where(on, code, 2)
    first = code & 1
    rise = (lax.shift_right_logical(code, 1) & 3) - 1
    second = lax.shift_right_logical(code, 3)
    group = lax.shift_right_logical(level, 3)
    span = (level & (GROUP - 1)) + 1
    row = group * COLS + second
    slot_a = first * depth + level
    first_column = first * FIRSTS[1]
    alone = (rise == 0) & (second == first_column)
    plans[0] = slot_a
    plans[1] = row * SPAN + span + rise
    plans[2] = jnp.where(on, slot_a, trash_a)
    plans[3] = jnp.where(on & jnp.logical_not(alone), row * 16 + span + rise, trash_b)
    plans[4] = (group * COLS + first_column) * SPAN + span
    copy = pltpu.make_async_copy(plans, codes, arrived)
    copy.start()
    top = lax.div(reach + (GROUP - 1), GROUP)

    zero = jnp.zeros((8, width), f32)
    one = jnp.ones((8, width), f32)
    for out in outs:
        out[...] = jnp.zeros(out.shape, f32)

    def put(block, row, value):
        stage[pl.ds((block * 16 + row) * 8, 8), :] = value

    for block in range(5):
        for row in range(16):
            put(block, row, zero)
    put(DIST, SQ, one * 0.25)
    put(CLOSE, VDOTR, -one)
    put(SUMS, 9, one)
    put(LEFT, ONE, one)

    rank = lax.broadcasted_iota(jnp.int32, (8, width), 0).astype(f32)

    def place(column, step, g, half):
        at = pl.ds(pl.multiple_of(g * 8 + half * 8, 8), 8)
        x = column[0, at, :] + (CELL * step[0] - 1.0)
        y = column[1, at, :] + (CELL * step[1] - 1.0)
        z = column[2, at, :] + (CELL * (rank + (half * 8 - 1.0)) - CELL * GROUP / 2)
        return x, y, z

    def prepare(g, carry):
        clear = jnp.zeros((COLS * 16, 16, width), f32)
        gsum[pl.ds(g * (COLS * 16), COLS * 16)] = clear
        ccol[pl.ds(g * (COLS * 16), COLS * 16)] = clear[:, 0:8]
        for base in (0, depth):
            fsum[pl.ds(base + g * 8, 8)] = clear[0:8]
            crow[pl.ds(base + g * 8, 8)] = jnp.zeros((8, width, width), f32)
        for c in range(COLS):
            for half in range(2):
                at = pl.ds(pl.multiple_of(g * 8 + half * 8, 8), 8)
                x, y, z = place(columns[c], STEPS[c], g, half)
                vx, vy, vz, rho, alive = [columns[c][n, at, :] for n in range(3, 8)]
                there = alive > 0.0
                square = x * x + y * y + z * z
                along = vx * x + vy * y + vz * z
                for n, (p, v) in enumerate(((x, vx), (y, vy), (z, vz))):
                    put(DIST, POS + n, -0.5 * p)
                    put(CLOSE, POS + n, v)
                    put(CLOSE, VEL + n, p)
                    high = p.astype(jnp.bfloat16).astype(f32)
                    mid = (p - high).astype(jnp.bfloat16).astype(f32)
                    put(SUMS, n, high)
                    put(SUMS, 3 + n, mid)
                    put(SUMS, 6 + n, p - high - mid)
                put(DIST, ONE, jnp.where(there, 0.25 * square, FAR))
                put(CLOSE, ONE, -along)
                push = stress(rho)
                put(FLAT, 0, 4.0 * rho)
                put(FLAT, 1, push)
                if c in FIRSTS:
                    for n, (p, v) in enumerate(((x, vx), (y, vy), (z, vz))):
                        put(LEFT, POS + n, p)
                        put(LEFT, VEL + n, v)
                    put(LEFT, SQ, jnp.where(there, square, 4.0 * FAR))
                    put(LEFT, VDOTR, along)
                for k in range(8 if half == 0 else 2):
                    slot = (g * COLS + c) * SPAN + half * 8 + k
                    high, mid, low = split(stage[pl.ds(k, 32, stride=8), :])
                    right[slot, 0] = high
                    right[slot, 1] = mid
                    right[slot, 2] = low
                    rows[slot] = stage[pl.ds(SUMS * 128 + k, 16, stride=8), :].astype(jnp.bfloat16)
                    sums = [stage[pl.ds(FLAT * 128 + row * 8 + k, 1), :] for row in range(2)]
                    for row in range(2):
                        flat_b[slot, row * 8:row * 8 + 8] = jnp.broadcast_to(sums[row], (8, width))
                    if c in FIRSTS and 1 <= half * 8 + k <= 8:
                        slot_a = FIRSTS.index(c) * depth + g * 8 + half * 8 + k - 1
                        h, m, l = [t.astype(f32) for t in split(stage[pl.ds(LEFT * 128 + k, 16, stride=8), :])]
                        wide = jnp.concatenate([h, h, h, m, m, l, m, l], 0)
                        left[slot_a] = wide.T.astype(jnp.bfloat16)
                        for row in range(2):
                            spread = jnp.broadcast_to(sums[row], (width, width)).T
                            flat_a[slot_a, row * width:row * width + width] = spread
        return carry

    lax.fori_loop(0, top, prepare, 0)

    def fetch(fields, block, u):
        n = (block + 1) * UNROLL + u
        return [codes[k, lax.shift_right_logical(n, 7), n & 127] for k in fields]

    def front(block, grids):
        for u in range(UNROLL):
            slot_a, slot_b = fetch((0, 1), block, u)
            pieces = []
            for out in range(2):
                h, m, l = [right[slot_b, s, out * 16:out * 16 + 16, :] for s in range(3)]
                pieces.append(jnp.concatenate([h, m, l, h, m, h, l, m], 0))
            grids[u] = jnp.dot(left[slot_a], jnp.concatenate(pieces, 1), preferred_element_type=f32)

    def middle(block, grids, highs, lows):
        for u in range(UNROLL):
            slot_a, slot_b, to_a, to_b = fetch((0, 1, 2, 3), block, u)
            rho_b = flat_b[slot_b, 0:8]
            push_b = flat_b[slot_b, 8:16]
            rho_b = jnp.concatenate([rho_b, rho_b], 0)
            push_b = jnp.concatenate([push_b, push_b], 0)
            colsum = None
            for r in range(0, width, 16):
                dist = jnp.maximum(grids[u, r:r + 16, 0:width], 1e-12)
                ncl = grids[u, r:r + 16, width:2 * width]
                denom = (dist + EPS / 4) * (flat_a[slot_a, r:r + 16] + rho_b)
                press = flat_a[slot_a, width + r:width + r + 16] + push_b
                reach = jnp.maximum(1.0 - dist * lax.rsqrt(dist), 0.0)
                weight = reach * reach * reach
                visc = jnp.maximum(ncl, 0.0) * pl.reciprocal(denom, approx=True)
                force = (press + visc) * weight
                change = ncl * weight
                high = force.astype(jnp.bfloat16)
                highs[u, r:r + 16] = high
                lows[u, r:r + 16] = (force - high.astype(f32)).astype(jnp.bfloat16)
                part = change[0:8] + change[8:16]
                colsum = part if colsum is None else colsum + part
                crow[to_a, r:r + 16, :] += change
            ccol[to_b] += colsum

    def reduce(block, highs, lows):
        for u in range(UNROLL):
            slot_b, to_a, to_b, own = fetch((1, 2, 3, 4), block, u)
            row_b = rows[slot_b]
            row_a = rows[own]
            high = highs[u]
            low = lows[u]
            fsum[to_a] += lax.dot_general(
                jnp.concatenate([row_b, row_b], 1), jnp.concatenate([high, low], 1),
                (((1,), (1,)), ((), ())), preferred_element_type=f32)
            gsum[to_b] += jnp.dot(
                jnp.concatenate([row_a, row_a], 1), jnp.concatenate([high, low], 0),
                preferred_element_type=f32)

    def advance(i, carry):
        front(2 * i + 1, grid1)
        middle(2 * i, grid0, high0, low0)
        reduce(2 * i - 1, high1, low1)
        front(2 * i + 2, grid0)
        middle(2 * i + 1, grid1, high1, low1)
        reduce(2 * i, high0, low0)
        return carry

    copy.wait()
    blocks = lax.div(live + (UNROLL - 1), UNROLL)
    front(0, grid0)
    lax.fori_loop(0, lax.div(blocks + 2, 2), advance, 0)

    def finish(g, carry):
        base = g * 8
        at1 = pl.ds(base + 1, 8)

        def levels(ref, start, row):
            return jnp.concatenate([ref[start + k, row:row + 1, :] for k in range(8)], 0)

        for n_first, c in enumerate(FIRSTS):
            start = n_first * depth + base
            for k in range(8):
                stage[pl.ds(k, 1), :] = jnp.sum(crow[start + k].T, axis=0, keepdims=True)
            x = columns[c][0, at1, :] + (CELL * STEPS[c][0] - 1.0)
            y = columns[c][1, at1, :] + (CELL * STEPS[c][1] - 1.0)
            z = columns[c][2, at1, :] + (CELL * rank - CELL * GROUP / 2)
            weight = levels(fsum, start, 9)
            for n, p in enumerate((x, y, z)):
                total_n = levels(fsum, start, n) + levels(fsum, start, 3 + n) + levels(fsum, start, 6 + n)
                outs[c][n, at1, :] += SCALE * (total_n - p * weight)
            outs[c][3, at1, :] += -SCALE * stage[pl.ds(0, 8), :]
        for c in range(COLS):
            for half in range(2):
                at = pl.ds(pl.multiple_of(base + half * 8, 8), 8)
                start = (g * COLS + c) * 16 + half * 8
                place_at = place(columns[c], STEPS[c], g, half)
                weight = levels(gsum, start, 9)
                for n, p in enumerate(place_at):
                    total_n = levels(gsum, start, n) + levels(gsum, start, 3 + n) + levels(gsum, start, 6 + n)
                    outs[c][n, at, :] += SCALE * (total_n - p * weight)
                moved = jnp.concatenate([jnp.sum(ccol[start + k], axis=0, keepdims=True) for k in range(8)], 0)
                outs[c][3, at, :] += -SCALE * moved
        return carry

    lax.fori_loop(0, top, finish, 0)
    inner = slice(1, depth + 1)
    own_force[...] = a0[0:3, inner, :]
    own_rate[...] = a0[3, inner, :]
    for out, sums in ((o1, a1), (o2, a2), (o3, a3)):
        out[...] = sums[:, inner, :]


def forces(before, columns, depth, width):
    groups = depth // GROUP
    levels = columns[0].shape[1]
    vmem = pl.BlockSpec(memory_space=pltpu.VMEM)
    slots = groups * COLS * SPAN
    sums = groups * COLS * 16 + 8
    f32, bf16 = jnp.float32, jnp.bfloat16
    return pl.pallas_call(
        functools.partial(kernel, width, depth),
        out_shape=[jax.ShapeDtypeStruct((3, depth, width), f32), jax.ShapeDtypeStruct((depth, width), f32)]
        + [jax.ShapeDtypeStruct((4, depth, width), f32)] * (COLS - 1),
        in_specs=[vmem] * (COLS + 1),
        out_specs=[vmem] * (COLS + 1),
        scratch_shapes=[
            pltpu.VMEM((5 * 16 * 8, width), f32),
            pltpu.VMEM((2 * depth, width, width), bf16),
            pltpu.VMEM((slots, 3, 32, width), bf16),
            pltpu.VMEM((slots, 16, width), bf16),
            pltpu.VMEM((2 * depth, 2 * width, width), f32),
            pltpu.VMEM((slots, 16, width), f32),
            pltpu.VMEM((2 * depth + 1, 16, width), f32),
            pltpu.VMEM((sums, 16, width), f32),
            pltpu.VMEM((2 * depth + 1, width, width), f32),
            pltpu.VMEM((sums, 8, width), f32),
        ] + [pltpu.VMEM((UNROLL, width, 2 * width), f32)] * 2
        + [pltpu.VMEM((UNROLL, width, width), bf16)] * 4
        + [pltpu.VMEM((4, levels, width), f32)] * COLS
        + [pltpu.VMEM((5, 16, 128), jnp.int32), pltpu.SMEM((5, 16, 128), jnp.int32), pltpu.SemaphoreType.DMA],
        compiler_params=pltpu.CompilerParams(vmem_limit_bytes=58 * 2**20),
        name="tile_pairs",
    )(before, *columns)


def local(offsets, velocities, density, tile_count, pair_tiles, pair_count):
    depth, width = density.shape[2:]
    count_x = lax.axis_size("gx")
    count_y = lax.axis_size("gy")
    counts = tile_count[0, 0]
    mask = (lax.broadcasted_iota(jnp.int32, (depth, width), 1) < counts[:, None]).astype(jnp.float32)
    own = jnp.concatenate([offsets[:, 0, 0], velocities[:, 0, 0], density[0, 0][None], mask[None]], 0)
    own = jnp.pad(own, ((0, 0), (1, NOTE - depth), (0, 0)))
    pairs = pair_count[0].astype(jnp.float32)
    noted = (lax.broadcasted_iota(jnp.int32, own.shape, 1) == NOTE) & (
        lax.broadcasted_iota(jnp.int32, own.shape, 0) == 0)
    own = jnp.where(noted, pairs, own)

    def device(x, y):
        return (x % count_x) * count_y + y

    def route(dx, dy):
        return [
            (device(x + dx, y + dy), device(x, y))
            for x in range(count_x)
            for y in range(count_y)
            if 0 <= y + dy < count_y
        ]

    def home(dx, dy):
        return [(target, source) for source, target in route(dx, dy)]

    columns = [own] + [lax.ppermute(own, ("gx", "gy"), route(dx, dy)) for dx, dy in STEPS[1:]]
    before = lax.ppermute(jnp.full((8, width), pairs), ("gx", "gy"), route(-1, 0))
    force, rate, *parts = forces(before, columns, depth, width)
    parts = [lax.ppermute(part, ("gx", "gy"), home(dx, dy)) for part, (dx, dy) in zip(parts, STEPS[1:])]
    force = force + (parts[0][0:3] + parts[1][0:3] + parts[2][0:3])
    rate = rate + (parts[0][3] + parts[1][3] + parts[2][3])
    return (force[:, None, None], rate[None, None])


def solution(mesh):
    return jax.shard_map(
        local,
        mesh=mesh,
        in_specs=(
            P(None, "gx", "gy", None, None),
            P(None, "gx", "gy", None, None),
            P("gx", "gy", None, None),
            P("gx", "gy", None),
            P(None, ("gx", "gy")),
            P(("gx", "gy")),
        ),
        out_specs=(P(None, "gx", "gy", None, None), P("gx", "gy", None, None)),
        check_vma=False,
    )
```

```python
import functools
import math

import jax
import jax.numpy as jnp
from jax import lax
from jax.experimental import pallas as pl
from jax.experimental.pallas import tpu as pltpu
from jax.sharding import PartitionSpec as P

CELL = 2.0
BULK = 25.0 / 7.0
SCALE = 0.0625 * -105.0 / (16.0 * math.pi)
EPS = 0.01
FAR = 1024.0

GROUP = 8
COLS = 4
SPAN = 10
STEPS = ((0, 0), (0, 1), (1, 0), (1, 1))
FIRSTS = (0, 2)
ACROSS = ((0, 0, 0), (0, 0, 1), (0, 1, -1), (0, 1, 0), (0, 1, 1))
AHEAD = tuple((n, c, dz) for n, c in ((0, 2), (0, 3), (1, 1)) for dz in (-1, 0, 1))
NEXT = tuple((1, c + 2, dz) for _, c, dz in ACROSS)
MARK = 39
NOTE = 71
UNROLL = 8

POS, VEL, SQ, VDOTR, ONE = 0, 3, 6, 7, 8
DIST, CLOSE, SUMS, LEFT, FLAT = range(5)


def split(x):
    high = x.astype(jnp.bfloat16)
    rest = x - high.astype(jnp.float32)
    mid = rest.astype(jnp.bfloat16)
    low = (rest - mid.astype(jnp.float32)).astype(jnp.bfloat16)
    return high, mid, low


def stress(rho):
    cube = rho * rho * rho
    return BULK * (cube * cube * rho - 1.0) / (rho * rho)


def kernel(width, depth, c0, c1, c2, c3, own_force, own_rate, o1, o2, o3,
           stage, left, right, rows, flat_a, flat_b, fsum, gsum, crow, ccol,
           grid0, grid1, high0, high1, low0, low1, a0, a1, a2, a3, plans, codes, arrived):
    columns = (c0, c1, c2, c3)
    outs = (a0, a1, a2, a3)
    groups = depth // GROUP
    trash_a = 2 * depth
    trash_b = groups * COLS * 16
    f32 = jnp.float32

    steps_up = lax.broadcasted_iota(jnp.int32, columns[0].shape[1:], 0).astype(f32)
    heights = [jnp.max(steps_up * columns[c][7]).astype(jnp.int32) for c in range(COLS)]
    here, after = [jnp.max(columns[c][0, NOTE:NOTE + 1, :]).astype(jnp.int32) for c in FIRSTS]

    def kept(height, work):
        return height - jnp.minimum(lax.div(jnp.maximum(work - MARK * depth // 4, 0), len(ACROSS)), height)

    keep, keep_next = kept(heights[0], here), kept(heights[2], after)

    place = (lax.broadcasted_iota(jnp.int32, (16, 128), 0) * 128
             + lax.broadcasted_iota(jnp.int32, (16, 128), 1) - UNROLL)
    live = jnp.int32(0)
    reach = jnp.int32(0)
    level = jnp.zeros_like(place)
    code = jnp.zeros_like(place)
    for names, low, high in ((ACROSS, 0, keep), (AHEAD, 0, depth), (NEXT, keep_next, depth)):
        for n, c, dz in names:
            start = jnp.maximum(low, max(-dz, 0))
            stop = jnp.minimum(jnp.minimum(high, heights[FIRSTS[n]]), heights[c] - dz)
            some = stop > start
            here_on = place >= live
            level = jnp.where(here_on, place + (start - live), level)
            code = jnp.where(here_on, c * 8 + (dz + 1) * 2 + n, code)
            live += jnp.where(some, stop - start, 0)
            reach = jnp.where(some, jnp.maximum(reach, stop), reach)
    on = (place >= 0) & (place < live)
    level = jnp.where(on, level, 0)
    code = jnp.where(on, code, 2)
    first = code & 1
    rise = (lax.shift_right_logical(code, 1) & 3) - 1
    second = lax.shift_right_logical(code, 3)
    group = lax.shift_right_logical(level, 3)
    span = (level & (GROUP - 1)) + 1
    row = group * COLS + second
    slot_a = first * depth + level
    first_column = first * FIRSTS[1]
    alone = (rise == 0) & (second == first_column)
    plans[0] = slot_a
    plans[1] = row * SPAN + span + rise
    plans[2] = jnp.where(on, slot_a, trash_a)
    plans[3] = jnp.where(on & jnp.logical_not(alone), row * 16 + span + rise, trash_b)
    plans[4] = (group * COLS + first_column) * SPAN + span
    copy = pltpu.make_async_copy(plans, codes, arrived)
    copy.start()
    top = lax.div(reach + (GROUP - 1), GROUP)

    zero = jnp.zeros((8, width), f32)
    one = jnp.ones((8, width), f32)
    for out in outs:
        out[...] = jnp.zeros(out.shape, f32)

    def put(block, row, value):
        stage[pl.ds((block * 16 + row) * 8, 8), :] = value

    for block in range(5):
        for row in range(16):
            put(block, row, zero)
    put(DIST, SQ, one * 0.25)
    put(CLOSE, VDOTR, -one)
    put(SUMS, 9, one)
    put(LEFT, ONE, one)

    rank = lax.broadcasted_iota(jnp.int32, (8, width), 0).astype(f32)

    def place(column, step, g, half):
        at = pl.ds(pl.multiple_of(g * 8 + half * 8, 8), 8)
        x = column[0, at, :] + (CELL * step[0] - 1.0)
        y = column[1, at, :] + (CELL * step[1] - 1.0)
        z = column[2, at, :] + (CELL * (rank + (half * 8 - 1.0)) - CELL * GROUP / 2)
        return x, y, z

    def prepare(g, carry):
        clear = jnp.zeros((COLS * 16, 16, width), f32)
        gsum[pl.ds(g * (COLS * 16), COLS * 16)] = clear
        ccol[pl.ds(g * (COLS * 16), COLS * 16)] = clear[:, 0:8]
        for base in (0, depth):
            fsum[pl.ds(base + g * 8, 8)] = clear[0:8]
            crow[pl.ds(base + g * 8, 8)] = jnp.zeros((8, width, width), f32)
        for c in range(COLS):
            for half in range(2):
                at = pl.ds(pl.multiple_of(g * 8 + half * 8, 8), 8)
                x, y, z = place(columns[c], STEPS[c], g, half)
                vx, vy, vz, rho, alive = [columns[c][n, at, :] for n in range(3, 8)]
                there = alive > 0.0
                square = x * x + y * y + z * z
                along = vx * x + vy * y + vz * z
                for n, (p, v) in enumerate(((x, vx), (y, vy), (z, vz))):
                    put(DIST, POS + n, -0.5 * p)
                    put(CLOSE, POS + n, v)
                    put(CLOSE, VEL + n, p)
                    high = p.astype(jnp.bfloat16).astype(f32)
                    mid = (p - high).astype(jnp.bfloat16).astype(f32)
                    put(SUMS, n, high)
                    put(SUMS, 3 + n, mid)
                    put(SUMS, 6 + n, p - high - mid)
                put(DIST, ONE, jnp.where(there, 0.25 * square, FAR))
                put(CLOSE, ONE, -along)
                push = stress(rho)
                put(FLAT, 0, 4.0 * rho)
                put(FLAT, 1, push)
                if c in FIRSTS:
                    for n, (p, v) in enumerate(((x, vx), (y, vy), (z, vz))):
                        put(LEFT, POS + n, p)
                        put(LEFT, VEL + n, v)
                    put(LEFT, SQ, jnp.where(there, square, 4.0 * FAR))
                    put(LEFT, VDOTR, along)
                for k in range(8 if half == 0 else 2):
                    slot = (g * COLS + c) * SPAN + half * 8 + k
                    high, mid, low = split(stage[pl.ds(k, 32, stride=8), :])
                    right[slot, 0] = high
                    right[slot, 1] = mid
                    right[slot, 2] = low
                    rows[slot] = stage[pl.ds(SUMS * 128 + k, 16, stride=8), :].astype(jnp.bfloat16)
                    sums = [stage[pl.ds(FLAT * 128 + row * 8 + k, 1), :] for row in range(2)]
                    for row in range(2):
                        flat_b[slot, row * 8:row * 8 + 8] = jnp.broadcast_to(sums[row], (8, width))
                    if c in FIRSTS and 1 <= half * 8 + k <= 8:
                        slot_a = FIRSTS.index(c) * depth + g * 8 + half * 8 + k - 1
                        h, m, l = [t.astype(f32) for t in split(stage[pl.ds(LEFT * 128 + k, 16, stride=8), :])]
                        wide = jnp.concatenate([h, h, h, m, m, l, m, l], 0)
                        left[slot_a] = wide.T.astype(jnp.bfloat16)
                        for row in range(2):
                            spread = jnp.broadcast_to(sums[row], (width, width)).T
                            flat_a[slot_a, row * width:row * width + width] = spread
        return carry

    lax.fori_loop(0, top, prepare, 0)

    def fetch(fields, block, u):
        n = (block + 1) * UNROLL + u
        return [codes[k, lax.shift_right_logical(n, 7), n & 127] for k in fields]

    def front(block, grids):
        for u in range(UNROLL):
            slot_a, slot_b = fetch((0, 1), block, u)
            pieces = []
            for out in range(2):
                h, m, l = [right[slot_b, s, out * 16:out * 16 + 16, :] for s in range(3)]
                pieces.append(jnp.concatenate([h, m, l, h, m, h, l, m], 0))
            grids[u] = jnp.dot(left[slot_a], jnp.concatenate(pieces, 1), preferred_element_type=f32)

    def middle(block, grids, highs, lows):
        for u in range(UNROLL):
            slot_a, slot_b, to_a, to_b = fetch((0, 1, 2, 3), block, u)
            rho_b = flat_b[slot_b, 0:8]
            push_b = flat_b[slot_b, 8:16]
            rho_b = jnp.concatenate([rho_b, rho_b], 0)
            push_b = jnp.concatenate([push_b, push_b], 0)
            colsum = None
            for r in range(0, width, 16):
                dist = jnp.maximum(grids[u, r:r + 16, 0:width], 1e-12)
                ncl = grids[u, r:r + 16, width:2 * width]
                denom = (dist + EPS / 4) * (flat_a[slot_a, r:r + 16] + rho_b)
                press = flat_a[slot_a, width + r:width + r + 16] + push_b
                reach = jnp.maximum(1.0 - dist * lax.rsqrt(dist), 0.0)
                weight = reach * reach * reach
                visc = jnp.maximum(ncl, 0.0) * pl.reciprocal(denom, approx=True)
                force = (press + visc) * weight
                change = ncl * weight
                high = force.astype(jnp.bfloat16)
                highs[u, r:r + 16] = high
                lows[u, r:r + 16] = (force - high.astype(f32)).astype(jnp.bfloat16)
                part = change[0:8] + change[8:16]
                colsum = part if colsum is None else colsum + part
                crow[to_a, r:r + 16, :] += change
            ccol[to_b] += colsum

    def reduce(block, highs, lows):
        for u in range(UNROLL):
            slot_b, to_a, to_b, own = fetch((1, 2, 3, 4), block, u)
            row_b = rows[slot_b]
            row_a = rows[own]
            high = highs[u]
            low = lows[u]
            fsum[to_a] += lax.dot_general(
                jnp.concatenate([row_b, row_b], 1), jnp.concatenate([high, low], 1),
                (((1,), (1,)), ((), ())), preferred_element_type=f32)
            gsum[to_b] += jnp.dot(
                jnp.concatenate([row_a, row_a], 1), jnp.concatenate([high, low], 0),
                preferred_element_type=f32)

    def advance(i, carry):
        front(2 * i + 1, grid1)
        middle(2 * i, grid0, high0, low0)
        reduce(2 * i - 1, high1, low1)
        front(2 * i + 2, grid0)
        middle(2 * i + 1, grid1, high1, low1)
        reduce(2 * i, high0, low0)
        return carry

    copy.wait()
    blocks = lax.div(live + (UNROLL - 1), UNROLL)
    front(0, grid0)
    lax.fori_loop(0, lax.div(blocks + 2, 2), advance, 0)

    def finish(g, carry):
        base = g * 8
        at1 = pl.ds(base + 1, 8)

        def levels(ref, start, row):
            return jnp.concatenate([ref[start + k, row:row + 1, :] for k in range(8)], 0)

        for n_first, c in enumerate(FIRSTS):
            start = n_first * depth + base
            for k in range(8):
                stage[pl.ds(k, 1), :] = jnp.sum(crow[start + k].T, axis=0, keepdims=True)
            x = columns[c][0, at1, :] + (CELL * STEPS[c][0] - 1.0)
            y = columns[c][1, at1, :] + (CELL * STEPS[c][1] - 1.0)
            z = columns[c][2, at1, :] + (CELL * rank - CELL * GROUP / 2)
            weight = levels(fsum, start, 9)
            for n, p in enumerate((x, y, z)):
                total_n = levels(fsum, start, n) + levels(fsum, start, 3 + n) + levels(fsum, start, 6 + n)
                outs[c][n, at1, :] += SCALE * (total_n - p * weight)
            outs[c][3, at1, :] += -SCALE * stage[pl.ds(0, 8), :]
        for c in range(COLS):
            for half in range(2):
                at = pl.ds(pl.multiple_of(base + half * 8, 8), 8)
                start = (g * COLS + c) * 16 + half * 8
                place_at = place(columns[c], STEPS[c], g, half)
                weight = levels(gsum, start, 9)
                for n, p in enumerate(place_at):
                    total_n = levels(gsum, start, n) + levels(gsum, start, 3 + n) + levels(gsum, start, 6 + n)
                    outs[c][n, at, :] += SCALE * (total_n - p * weight)
                moved = jnp.concatenate([jnp.sum(ccol[start + k], axis=0, keepdims=True) for k in range(8)], 0)
                outs[c][3, at, :] += -SCALE * moved
        return carry

    lax.fori_loop(0, top, finish, 0)
    inner = slice(1, depth + 1)
    own_force[...] = a0[0:3, inner, :]
    own_rate[...] = a0[3, inner, :]
    for out, sums in ((o1, a1), (o2, a2), (o3, a3)):
        out[...] = sums[:, inner, :]


def forces(columns, depth, width):
    groups = depth // GROUP
    levels = columns[0].shape[1]
    vmem = pl.BlockSpec(memory_space=pltpu.VMEM)
    slots = groups * COLS * SPAN
    sums = groups * COLS * 16 + 8
    f32, bf16 = jnp.float32, jnp.bfloat16
    return pl.pallas_call(
        functools.partial(kernel, width, depth),
        out_shape=[jax.ShapeDtypeStruct((3, depth, width), f32), jax.ShapeDtypeStruct((depth, width), f32)]
        + [jax.ShapeDtypeStruct((4, depth, width), f32)] * (COLS - 1),
        in_specs=[vmem] * COLS,
        out_specs=[vmem] * (COLS + 1),
        scratch_shapes=[
            pltpu.VMEM((5 * 16 * 8, width), f32),
            pltpu.VMEM((2 * depth, width, width), bf16),
            pltpu.VMEM((slots, 3, 32, width), bf16),
            pltpu.VMEM((slots, 16, width), bf16),
            pltpu.VMEM((2 * depth, 2 * width, width), f32),
            pltpu.VMEM((slots, 16, width), f32),
            pltpu.VMEM((2 * depth + 1, 16, width), f32),
            pltpu.VMEM((sums, 16, width), f32),
            pltpu.VMEM((2 * depth + 1, width, width), f32),
            pltpu.VMEM((sums, 8, width), f32),
        ] + [pltpu.VMEM((UNROLL, width, 2 * width), f32)] * 2
        + [pltpu.VMEM((UNROLL, width, width), bf16)] * 4
        + [pltpu.VMEM((4, levels, width), f32)] * COLS
        + [pltpu.VMEM((5, 16, 128), jnp.int32), pltpu.SMEM((5, 16, 128), jnp.int32), pltpu.SemaphoreType.DMA],
        compiler_params=pltpu.CompilerParams(vmem_limit_bytes=58 * 2**20),
        name="tile_pairs",
    )(*columns)


def local(offsets, velocities, density, tile_count, pair_tiles, pair_count):
    depth, width = density.shape[2:]
    count_x = lax.axis_size("gx")
    count_y = lax.axis_size("gy")
    counts = tile_count[0, 0]
    mask = (lax.broadcasted_iota(jnp.int32, (depth, width), 1) < counts[:, None]).astype(jnp.float32)
    own = jnp.concatenate([offsets[:, 0, 0], velocities[:, 0, 0], density[0, 0][None], mask[None]], 0)
    own = jnp.pad(own, ((0, 0), (1, NOTE - depth), (0, 0)))
    edge = jnp.where(lax.axis_index("gy") == 0, 3 * depth, 0)
    pairs = (pair_count[0] + edge).astype(jnp.float32)
    noted = (lax.broadcasted_iota(jnp.int32, own.shape, 1) == NOTE) & (
        lax.broadcasted_iota(jnp.int32, own.shape, 0) == 0)
    own = jnp.where(noted, pairs, own)

    def device(x, y):
        return (x % count_x) * count_y + y

    def route(dx, dy):
        return [
            (device(x + dx, y + dy), device(x, y))
            for x in range(count_x)
            for y in range(count_y)
            if 0 <= y + dy < count_y
        ]

    def home(dx, dy):
        return [(target, source) for source, target in route(dx, dy)]

    columns = [own] + [lax.ppermute(own, ("gx", "gy"), route(dx, dy)) for dx, dy in STEPS[1:]]
    force, rate, *parts = forces(columns, depth, width)
    parts = [lax.ppermute(part, ("gx", "gy"), home(dx, dy)) for part, (dx, dy) in zip(parts, STEPS[1:])]
    force = force + (parts[0][0:3] + parts[1][0:3] + parts[2][0:3])
    rate = rate + (parts[0][3] + parts[1][3] + parts[2][3])
    return (force[:, None, None], rate[None, None])


def solution(mesh):
    return jax.shard_map(
        local,
        mesh=mesh,
        in_specs=(
            P(None, "gx", "gy", None, None),
            P(None, "gx", "gy", None, None),
            P("gx", "gy", None, None),
            P("gx", "gy", None),
            P(None, ("gx", "gy")),
            P(("gx", "gy")),
        ),
        out_specs=(P(None, "gx", "gy", None, None), P("gx", "gy", None, None)),
        check_vma=False,
    )
```

```python
import functools
import math

import jax
import jax.numpy as jnp
from jax import lax
from jax.experimental import pallas as pl
from jax.experimental.pallas import tpu as pltpu
from jax.sharding import PartitionSpec as P

CELL = 2.0
BULK = 25.0 / 7.0
SCALE = 0.0625 * -105.0 / (16.0 * math.pi)
EPS = 0.01
FAR = 1024.0

GROUP = 8
COLS = 4
SPAN = 10
STEPS = ((0, 0), (0, 1), (1, 0), (1, 1))
FIRSTS = (0, 2)
ACROSS = ((0, 0, 0), (0, 0, 1), (0, 1, -1), (0, 1, 0), (0, 1, 1))
AHEAD = tuple((n, c, dz) for n, c in ((0, 2), (0, 3), (1, 1)) for dz in (-1, 0, 1))
NEXT = tuple((1, c + 2, dz) for _, c, dz in ACROSS)
MARK = 39
NOTE = 71
UNROLL = 8

POS, VEL, SQ, VDOTR, ONE = 0, 3, 6, 7, 8
DIST, CLOSE, SUMS, LEFT, FLAT = range(5)


def split(x):
    high = x.astype(jnp.bfloat16)
    rest = x - high.astype(jnp.float32)
    mid = rest.astype(jnp.bfloat16)
    low = (rest - mid.astype(jnp.float32)).astype(jnp.bfloat16)
    return high, mid, low


def stress(rho):
    cube = rho * rho * rho
    return BULK * (cube * cube * rho - 1.0) / (rho * rho)


def kernel(width, depth, c0, c1, c2, c3, own_force, own_rate, o1, o2, o3,
           stage, left, right, rows, flat_a, flat_b, fsum, gsum, crow, ccol,
           grid0, grid1, high0, high1, low0, low1, a0, a1, a2, a3, plans, codes, arrived):
    columns = (c0, c1, c2, c3)
    outs = (a0, a1, a2, a3)
    groups = depth // GROUP
    trash_a = 2 * depth
    trash_b = groups * COLS * 16
    f32 = jnp.float32

    steps_up = lax.broadcasted_iota(jnp.int32, columns[0].shape[1:], 0).astype(f32)
    heights = [jnp.max(steps_up * columns[c][7]).astype(jnp.int32) for c in range(COLS)]
    here, after = [jnp.max(columns[c][0, NOTE:NOTE + 1, :]).astype(jnp.int32) for c in FIRSTS]

    def kept(height, work):
        return height - jnp.minimum(lax.div(jnp.maximum(work - MARK * depth // 4, 0), len(ACROSS)), height)

    keep, keep_next = kept(heights[0], here), kept(heights[2], after)

    place = (lax.broadcasted_iota(jnp.int32, (16, 128), 0) * 128
             + lax.broadcasted_iota(jnp.int32, (16, 128), 1) - UNROLL)
    live = jnp.int32(0)
    reach = jnp.int32(0)
    level = jnp.zeros_like(place)
    code = jnp.zeros_like(place)
    for names, low, high in ((ACROSS, 0, keep), (AHEAD, 0, depth), (NEXT, keep_next, depth)):
        for n, c, dz in names:
            start = jnp.maximum(low, max(-dz, 0))
            stop = jnp.minimum(jnp.minimum(high, heights[FIRSTS[n]]), heights[c] - dz)
            some = stop > start
            here_on = place >= live
            level = jnp.where(here_on, place + (start - live), level)
            code = jnp.where(here_on, c * 8 + (dz + 1) * 2 + n, code)
            live += jnp.where(some, stop - start, 0)
            reach = jnp.where(some, jnp.maximum(reach, stop), reach)
    on = (place >= 0) & (place < live)
    level = jnp.where(on, level, 0)
    code = jnp.where(on, code, 2)
    first = code & 1
    rise = (lax.shift_right_logical(code, 1) & 3) - 1
    second = lax.shift_right_logical(code, 3)
    group = lax.shift_right_logical(level, 3)
    span = (level & (GROUP - 1)) + 1
    row = group * COLS + second
    slot_a = first * depth + level
    first_column = first * FIRSTS[1]
    alone = (rise == 0) & (second == first_column)
    plans[0] = slot_a
    plans[1] = row * SPAN + span + rise
    plans[2] = jnp.where(on, slot_a, trash_a)
    plans[3] = jnp.where(on & jnp.logical_not(alone), row * 16 + span + rise, trash_b)
    plans[4] = (group * COLS + first_column) * SPAN + span
    copy = pltpu.make_async_copy(plans, codes, arrived)
    copy.start()
    top = lax.div(reach + (GROUP - 1), GROUP)

    zero = jnp.zeros((8, width), f32)
    one = jnp.ones((8, width), f32)
    for out in outs:
        out[...] = jnp.zeros(out.shape, f32)

    def put(block, row, value):
        stage[pl.ds((block * 16 + row) * 8, 8), :] = value

    for block in range(5):
        for row in range(16):
            put(block, row, zero)
    put(DIST, SQ, one * 0.25)
    put(CLOSE, VDOTR, -one)
    put(SUMS, 9, one)
    put(LEFT, ONE, one)

    rank = lax.broadcasted_iota(jnp.int32, (8, width), 0).astype(f32)

    def place(column, step, g, half):
        at = pl.ds(pl.multiple_of(g * 8 + half * 8, 8), 8)
        x = column[0, at, :] + (CELL * step[0] - 1.0)
        y = column[1, at, :] + (CELL * step[1] - 1.0)
        z = column[2, at, :] + (CELL * (rank + (half * 8 - 1.0)) - CELL * GROUP / 2)
        return x, y, z

    def prepare(g, carry):
        clear = jnp.zeros((COLS * 16, 16, width), f32)
        gsum[pl.ds(g * (COLS * 16), COLS * 16)] = clear
        ccol[pl.ds(g * (COLS * 16), COLS * 16)] = clear[:, 0:8]
        for base in (0, depth):
            fsum[pl.ds(base + g * 8, 8)] = clear[0:8]
            crow[pl.ds(base + g * 8, 8)] = jnp.zeros((8, width, width), f32)
        for c in range(COLS):
            for half in range(2):
                at = pl.ds(pl.multiple_of(g * 8 + half * 8, 8), 8)
                x, y, z = place(columns[c], STEPS[c], g, half)
                vx, vy, vz, rho, alive = [columns[c][n, at, :] for n in range(3, 8)]
                there = alive > 0.0
                square = x * x + y * y + z * z
                along = vx * x + vy * y + vz * z
                for n, (p, v) in enumerate(((x, vx), (y, vy), (z, vz))):
                    put(DIST, POS + n, -0.5 * p)
                    put(CLOSE, POS + n, v)
                    put(CLOSE, VEL + n, p)
                    high = p.astype(jnp.bfloat16).astype(f32)
                    mid = (p - high).astype(jnp.bfloat16).astype(f32)
                    put(SUMS, n, high)
                    put(SUMS, 3 + n, mid)
                    put(SUMS, 6 + n, p - high - mid)
                put(DIST, ONE, jnp.where(there, 0.25 * square, FAR))
                put(CLOSE, ONE, -along)
                push = stress(rho)
                put(FLAT, 0, 4.0 * rho)
                put(FLAT, 1, push)
                if c in FIRSTS:
                    for n, (p, v) in enumerate(((x, vx), (y, vy), (z, vz))):
                        put(LEFT, POS + n, p)
                        put(LEFT, VEL + n, v)
                    put(LEFT, SQ, jnp.where(there, square, 4.0 * FAR))
                    put(LEFT, VDOTR, along)
                for k in range(8 if half == 0 else 2):
                    slot = (g * COLS + c) * SPAN + half * 8 + k
                    high, mid, low = split(stage[pl.ds(k, 32, stride=8), :])
                    right[slot, 0] = high
                    right[slot, 1] = mid
                    right[slot, 2] = low
                    rows[slot] = stage[pl.ds(SUMS * 128 + k, 16, stride=8), :].astype(jnp.bfloat16)
                    sums = [stage[pl.ds(FLAT * 128 + row * 8 + k, 1), :] for row in range(2)]
                    for row in range(2):
                        flat_b[slot, row * 8:row * 8 + 8] = jnp.broadcast_to(sums[row], (8, width))
                    if c in FIRSTS and 1 <= half * 8 + k <= 8:
                        slot_a = FIRSTS.index(c) * depth + g * 8 + half * 8 + k - 1
                        h, m, l = [t.astype(f32) for t in split(stage[pl.ds(LEFT * 128 + k, 16, stride=8), :])]
                        wide = jnp.concatenate([h, h, h, m, m, l, m, l], 0)
                        left[slot_a] = wide.T.astype(jnp.bfloat16)
                        for row in range(2):
                            spread = jnp.broadcast_to(sums[row], (width, width)).T
                            flat_a[slot_a, row * width:row * width + width] = spread
        return carry

    lax.fori_loop(0, top, prepare, 0)

    def fetch(fields, block, u):
        n = (block + 1) * UNROLL + u
        return [codes[k, lax.shift_right_logical(n, 7), n & 127] for k in fields]

    def front(block, grids):
        for u in range(UNROLL):
            slot_a, slot_b = fetch((0, 1), block, u)
            pieces = []
            for out in range(2):
                h, m, l = [right[slot_b, s, out * 16:out * 16 + 16, :] for s in range(3)]
                pieces.append(jnp.concatenate([h, m, l, h, m, h, l, m], 0))
            grids[u] = jnp.dot(left[slot_a], jnp.concatenate(pieces, 1), preferred_element_type=f32)

    def middle(block, grids, highs, lows):
        for u in range(UNROLL):
            slot_a, slot_b, to_a, to_b = fetch((0, 1, 2, 3), block, u)
            rho_b = flat_b[slot_b, 0:8]
            push_b = flat_b[slot_b, 8:16]
            rho_b = jnp.concatenate([rho_b, rho_b], 0)
            push_b = jnp.concatenate([push_b, push_b], 0)
            colsum = None
            for r in range(0, width, 16):
                dist = jnp.maximum(grids[u, r:r + 16, 0:width], 1e-12)
                ncl = grids[u, r:r + 16, width:2 * width]
                denom = (dist + EPS / 4) * (flat_a[slot_a, r:r + 16] + rho_b)
                press = flat_a[slot_a, width + r:width + r + 16] + push_b
                reach = jnp.maximum(1.0 - dist * lax.rsqrt(dist), 0.0)
                weight = reach * reach * reach
                visc = jnp.maximum(ncl, 0.0) * pl.reciprocal(denom, approx=True)
                force = (press + visc) * weight
                change = ncl * weight
                high = force.astype(jnp.bfloat16)
                highs[u, r:r + 16] = high
                lows[u, r:r + 16] = (force - high.astype(f32)).astype(jnp.bfloat16)
                part = change[0:8] + change[8:16]
                colsum = part if colsum is None else colsum + part
                crow[to_a, r:r + 16, :] += change
            ccol[to_b] += colsum

    def reduce(block, highs, lows):
        for u in range(UNROLL):
            slot_b, to_a, to_b, own = fetch((1, 2, 3, 4), block, u)
            row_b = rows[slot_b]
            row_a = rows[own]
            high = highs[u]
            low = lows[u]
            fsum[to_a] += lax.dot_general(
                jnp.concatenate([row_b, row_b], 1), jnp.concatenate([high, low], 1),
                (((1,), (1,)), ((), ())), preferred_element_type=f32)
            gsum[to_b] += jnp.dot(
                jnp.concatenate([row_a, row_a], 1), jnp.concatenate([high, low], 0),
                preferred_element_type=f32)

    def advance(i, carry):
        front(2 * i + 1, grid1)
        middle(2 * i, grid0, high0, low0)
        reduce(2 * i - 1, high1, low1)
        front(2 * i + 2, grid0)
        middle(2 * i + 1, grid1, high1, low1)
        reduce(2 * i, high0, low0)
        return carry

    copy.wait()
    blocks = lax.div(live + (UNROLL - 1), UNROLL)
    front(0, grid0)
    lax.fori_loop(0, lax.div(blocks + 2, 2), advance, 0)

    def finish(g, carry):
        base = g * 8
        at1 = pl.ds(base + 1, 8)

        def levels(ref, start, row):
            return jnp.concatenate([ref[start + k, row:row + 1, :] for k in range(8)], 0)

        for n_first, c in enumerate(FIRSTS):
            start = n_first * depth + base
            for k in range(8):
                stage[pl.ds(k, 1), :] = jnp.sum(crow[start + k].T, axis=0, keepdims=True)
            x = columns[c][0, at1, :] + (CELL * STEPS[c][0] - 1.0)
            y = columns[c][1, at1, :] + (CELL * STEPS[c][1] - 1.0)
            z = columns[c][2, at1, :] + (CELL * rank - CELL * GROUP / 2)
            weight = levels(fsum, start, 9)
            for n, p in enumerate((x, y, z)):
                total_n = levels(fsum, start, n) + levels(fsum, start, 3 + n) + levels(fsum, start, 6 + n)
                outs[c][n, at1, :] += SCALE * (total_n - p * weight)
            outs[c][3, at1, :] += -SCALE * stage[pl.ds(0, 8), :]
        for c in range(COLS):
            for half in range(2):
                at = pl.ds(pl.multiple_of(base + half * 8, 8), 8)
                start = (g * COLS + c) * 16 + half * 8
                place_at = place(columns[c], STEPS[c], g, half)
                weight = levels(gsum, start, 9)
                for n, p in enumerate(place_at):
                    total_n = levels(gsum, start, n) + levels(gsum, start, 3 + n) + levels(gsum, start, 6 + n)
                    outs[c][n, at, :] += SCALE * (total_n - p * weight)
                moved = jnp.concatenate([jnp.sum(ccol[start + k], axis=0, keepdims=True) for k in range(8)], 0)
                outs[c][3, at, :] += -SCALE * moved
        return carry

    lax.fori_loop(0, top, finish, 0)
    inner = slice(1, depth + 1)
    own_force[...] = a0[0:3, inner, :]
    own_rate[...] = a0[3, inner, :]
    for out, sums in ((o1, a1), (o2, a2), (o3, a3)):
        out[...] = sums[:, inner, :]


def forces(columns, depth, width):
    groups = depth // GROUP
    levels = columns[0].shape[1]
    vmem = pl.BlockSpec(memory_space=pltpu.VMEM)
    slots = groups * COLS * SPAN
    sums = groups * COLS * 16 + 8
    f32, bf16 = jnp.float32, jnp.bfloat16
    return pl.pallas_call(
        functools.partial(kernel, width, depth),
        out_shape=[jax.ShapeDtypeStruct((3, depth, width), f32), jax.ShapeDtypeStruct((depth, width), f32)]
        + [jax.ShapeDtypeStruct((4, depth, width), f32)] * (COLS - 1),
        in_specs=[vmem] * COLS,
        out_specs=[vmem] * (COLS + 1),
        scratch_shapes=[
            pltpu.VMEM((5 * 16 * 8, width), f32),
            pltpu.VMEM((2 * depth, width, width), bf16),
            pltpu.VMEM((slots, 3, 32, width), bf16),
            pltpu.VMEM((slots, 16, width), bf16),
            pltpu.VMEM((2 * depth, 2 * width, width), f32),
            pltpu.VMEM((slots, 16, width), f32),
            pltpu.VMEM((2 * depth + 1, 16, width), f32),
            pltpu.VMEM((sums, 16, width), f32),
            pltpu.VMEM((2 * depth + 1, width, width), f32),
            pltpu.VMEM((sums, 8, width), f32),
        ] + [pltpu.VMEM((UNROLL, width, 2 * width), f32)] * 2
        + [pltpu.VMEM((UNROLL, width, width), bf16)] * 4
        + [pltpu.VMEM((4, levels, width), f32)] * COLS
        + [pltpu.VMEM((5, 16, 128), jnp.int32), pltpu.SMEM((5, 16, 128), jnp.int32), pltpu.SemaphoreType.DMA],
        compiler_params=pltpu.CompilerParams(vmem_limit_bytes=63 * 2**20),
        name="tile_pairs",
    )(*columns)


def local(offsets, velocities, density, tile_count, pair_tiles, pair_count):
    depth, width = density.shape[2:]
    count_x = lax.axis_size("gx")
    count_y = lax.axis_size("gy")
    counts = tile_count[0, 0]
    mask = (lax.broadcasted_iota(jnp.int32, (depth, width), 1) < counts[:, None]).astype(jnp.float32)
    own = jnp.concatenate([offsets[:, 0, 0], velocities[:, 0, 0], density[0, 0][None], mask[None]], 0)
    own = jnp.pad(own, ((0, 0), (1, NOTE - depth), (0, 0)))
    edge = jnp.where(lax.axis_index("gy") == 0, 3 * depth, 0)
    pairs = (pair_count[0] + edge).astype(jnp.float32)
    noted = (lax.broadcasted_iota(jnp.int32, own.shape, 1) == NOTE) & (
        lax.broadcasted_iota(jnp.int32, own.shape, 0) == 0)
    own = jnp.where(noted, pairs, own)

    def device(x, y):
        return (x % count_x) * count_y + y

    def route(dx, dy):
        return [
            (device(x + dx, y + dy), device(x, y))
            for x in range(count_x)
            for y in range(count_y)
            if 0 <= y + dy < count_y
        ]

    def home(dx, dy):
        return [(target, source) for source, target in route(dx, dy)]

    columns = [own] + [lax.ppermute(own, ("gx", "gy"), route(dx, dy)) for dx, dy in STEPS[1:]]
    force, rate, *parts = forces(columns, depth, width)
    parts = [lax.ppermute(part, ("gx", "gy"), home(dx, dy)) for part, (dx, dy) in zip(parts, STEPS[1:])]
    force = force + (parts[0][0:3] + parts[1][0:3] + parts[2][0:3])
    rate = rate + (parts[0][3] + parts[1][3] + parts[2][3])
    return (force[:, None, None], rate[None, None])


def solution(mesh):
    return jax.shard_map(
        local,
        mesh=mesh,
        in_specs=(
            P(None, "gx", "gy", None, None),
            P(None, "gx", "gy", None, None),
            P("gx", "gy", None, None),
            P("gx", "gy", None),
            P(None, ("gx", "gy")),
            P(("gx", "gy")),
        ),
        out_specs=(P(None, "gx", "gy", None, None), P("gx", "gy", None, None)),
        check_vma=False,
    )
```
